32 devices in a mesh: tok: 4 (over x, core), feat: 4 (over z), row: 2 (over y).
Axes of the slice: x: 2, y: 2, z: 4, core: 2. Of those that a mesh axis runs over, the one named last changes fastest.
Arguments:
- quantized: bfloat16 [16384, 28672], P('tok', 'feat'), may hold values from -8 to 8
- exponents: int32 [16384, 224], P('tok', 'feat'), may hold values from -3 to 3
- weights: bfloat16 [8192, 28672], P(('tok', 'row'), 'feat'), may hold values from -6 to 6
- keep_mask: int32 [8192, 256], P(('tok', 'row')), may hold values from 0 to 1, as said below
Outputs:
- pruned: bfloat16 [8192, 28672], P(('tok', 'row'), 'feat')
The draws below stay inside these ranges and needn't reach their ends.
Inputs may be any that keep to these rules, and one draw needn't show every extreme that they name: `keep_mask`: in every row each group of four consecutive columns holds exactly two ones.
All inputs are finite; a program needn't handle non-finite values.
Results may differ from the reference program's by a relative error of at most 0.0012.
Values may be sent and summed in bfloat16 or wider, within the bound.
No kernel may reach another device: no remote copies, remote signals or barrier semaphores. Data moves between devices by JAX's collectives and lax.ppermute only.
A program may use at most 256 MiB of HBM per device.

```python
import math
import jax
import jax.numpy as jnp
from jax import lax

ROWS = 8192
FF = 28672
PANEL = 256
QBLOCK = 128
TOKENS = 16384


def draw_keep_mask(key, part):
    scores = jax.random.randint(key, (ROWS, PANEL // 4, 4), 0, 1 << 20) * 4 + jnp.arange(4, dtype=jnp.int32)
    ranks = jnp.argsort(jnp.argsort(scores, axis=-1, stable=True), axis=-1, stable=True)
    return (ranks < 2).astype(jnp.int32).reshape(ROWS, PANEL)


def draw_quantized(key, part):
    shared_count = max(PANEL // 4, 2)
    noise_key = jax.random.fold_in(key, 101)
    token_key = jax.random.fold_in(key, 202)
    feature_key = jax.random.fold_in(key, 303)
    noise = jax.random.normal(noise_key, (TOKENS, FF), jnp.float32)
    token_factor = jax.random.normal(token_key, (TOKENS, shared_count), jnp.float32)
    feature_factor = jax.random.normal(feature_key, (shared_count, FF), jnp.float32) / math.sqrt(shared_count)
    common = jnp.dot(token_factor, feature_factor, precision=lax.Precision.HIGHEST)
    return jnp.clip(noise + common, -8.0, 8.0).astype(jnp.bfloat16)


def with_ends(drawn, key, low, high):
    spot = [jax.random.randint(jax.random.fold_in(key, axis), (), 0, length) for axis, length in enumerate(drawn.shape)]
    widest = drawn.shape.index(max(drawn.shape))
    neighbour = spot[:widest] + [(spot[widest] + 1) % drawn.shape[widest]] + spot[widest + 1:]
    return drawn.at[tuple(spot)].set(low).at[tuple(neighbour)].set(high)


def level_of(stream_key, shape, pieces, low, high):
    def one(position, parts):
        heights = jax.random.uniform(jax.random.fold_in(jax.random.fold_in(stream_key, 6), position), (parts,), jnp.float32, low / len(pieces), high / len(pieces))
        return jnp.repeat(jnp.exp(heights), shape[position] // parts).reshape((-1,) + (1,) * (len(shape) - position - 1))

    level = one(*pieces[0])
    for cut in pieces[1:]:
        level = level * one(*cut)
    return level


def bell_draw(stream_key, dims, deviation, limit, split=(), held_as=jnp.bfloat16):
    gain = level_of(stream_key, dims, split, -0.22, 0.18) if split else 1.0
    values = jax.random.normal(stream_key, dims, jnp.float32) * deviation * gain
    return jnp.minimum(jnp.maximum(values, -limit), limit).astype(held_as)


def setup_inputs(seed: int = 0) -> dict:
    arg_keys = jax.random.split(jax.random.key(seed), 5)
    quantized = draw_quantized(jax.random.fold_in(arg_keys[4], 71), 0)
    exponents = with_ends(jax.random.randint(arg_keys[1], (TOKENS, FF // QBLOCK), -3, 4), jax.random.fold_in(arg_keys[1], 1), -3, 3).astype(jnp.int32)
    weights = bell_draw(arg_keys[2], (ROWS, FF), 1.0, 6.0, ((0, 8), (1, 4)))
    keep_mask = draw_keep_mask(jax.random.fold_in(arg_keys[4], 71), 0)
    return dict(quantized=quantized, exponents=exponents, weights=weights, keep_mask=keep_mask)


def matmul_high(left, right):
    return jnp.dot(left, right, precision=lax.Precision.HIGHEST)

def factor_small(block):
    size = block.shape[0]
    lower = jnp.zeros_like(block)
    for j in range(size):
        head = lower[j, :j]
        diag_value = jnp.sqrt(block[j, j] - jnp.sum(head * head))
        column = (block[j:, j] - matmul_high(lower[j:, :j], head)) / diag_value
        lower = lower.at[j:, j].set(column)
    ident = jnp.eye(size, dtype=block.dtype)
    inverse = jnp.zeros_like(block)
    for i in range(size):
        row_value = (ident[i] - matmul_high(lower[i, :i], inverse[:i, :])) / lower[i, i]
        inverse = inverse.at[i].set(row_value)
    return (lower, inverse)

def factor_with_inverse(block):
    size = block.shape[0]
    if size <= 16:
        return factor_small(block)
    half = size // 2
    upper_lower, upper_inverse = factor_with_inverse(block[:half, :half])
    below = matmul_high(block[half:, :half], upper_inverse.T)
    rest = block[half:, half:] - matmul_high(below, below.T)
    rest_lower, rest_inverse = factor_with_inverse(rest)
    zeros_top = jnp.zeros((half, size - half), block.dtype)
    lower = jnp.concatenate([jnp.concatenate([upper_lower, zeros_top], axis=1), jnp.concatenate([below, rest_lower], axis=1)], axis=0)
    cross = -matmul_high(rest_inverse, matmul_high(below, upper_inverse))
    inverse = jnp.concatenate([jnp.concatenate([upper_inverse, zeros_top], axis=1), jnp.concatenate([cross, rest_inverse], axis=1)], axis=0)
    return (lower, inverse)

def reference(quantized, exponents, weights, keep_mask):
    tokens = quantized.shape[0]
    scales = jnp.exp2(exponents.astype(jnp.float32)).astype(jnp.bfloat16)
    activations = (quantized.reshape(tokens, FF // QBLOCK, QBLOCK) * scales[:, :, None]).reshape(tokens, FF)
    panel_acts = activations[:, :PANEL]
    hessian_panel = lax.dot_general(activations, panel_acts, (((0,), (0,)), ((), ())), preferred_element_type=jnp.float32)
    head_block = hessian_panel[:PANEL]
    damping = 0.01 * jnp.mean(jnp.diagonal(head_block))
    diag_block = head_block + damping * jnp.eye(PANEL, dtype=jnp.float32)
    factor, factor_inv = factor_with_inverse(diag_block)
    mask_float = keep_mask.astype(jnp.float32)
    pruned_error = weights[:, :PANEL].astype(jnp.float32) * (1.0 - mask_float)
    coefficients = matmul_high(matmul_high(pruned_error, factor_inv.T), factor_inv)
    update = jnp.dot(coefficients, hessian_panel.T, precision=lax.Precision.HIGHEST)
    columns = jnp.arange(FF)[None, :]
    masked = jnp.zeros((weights.shape[0], FF), jnp.float32).at[:, :PANEL].set(weights[:, :PANEL].astype(jnp.float32) * mask_float)
    result = jnp.where(columns < PANEL, masked, weights.astype(jnp.float32) + update)
    return result.astype(jnp.bfloat16)
```

```python
import functools

import jax
import jax.numpy as jnp
from jax import lax
from jax.experimental import pallas as pl
from jax.experimental.pallas import tpu as pltpu
from jax.sharding import PartitionSpec as P

PANEL = 256
QBLOCK = 128
CHUNKS = 4
F32 = jnp.float32
BF16 = jnp.bfloat16


def dot_high(left, right):
    return jnp.dot(left, right, precision=lax.Precision.HIGHEST, preferred_element_type=F32)


def gram_kernel(blocks, place_ref, quant_ref, scale_ref, panel_ref, out_ref, acts_ref):
    col = place_ref[0]
    shift = lax.rem(QBLOCK - lax.rem(col * blocks, QBLOCK), QBLOCK)
    scale = pltpu.roll(scale_ref[...], shift, 1)
    rows = scale.shape[0]
    for c in range(blocks):
        span = slice(c * QBLOCK, (c + 1) * QBLOCK)
        wide = jnp.broadcast_to(scale[:, c : c + 1], (rows, QBLOCK)).astype(BF16)
        acts_ref[:, span] = quant_ref[:, span] * wide
    part = jnp.dot(panel_ref[...], acts_ref[...], preferred_element_type=F32)

    @pl.when(pl.program_id(0) == 0)
    def _():
        out_ref[...] = part

    @pl.when(pl.program_id(0) > 0)
    def _():
        out_ref[...] += part


def gram_block(quantized, scale_pad, panel_t, col, width):
    tokens, cols = quantized.shape
    if width % QBLOCK or cols // QBLOCK > QBLOCK:
        quant = lax.dynamic_slice_in_dim(quantized, col * width, width, 1)
        index = (col * width + jnp.arange(width)) // QBLOCK
        acts = quant * jnp.take(scale_pad, index, axis=1).astype(BF16)
        return jnp.dot(panel_t, acts, preferred_element_type=F32)
    step = min(tokens, 1024)
    return pl.pallas_call(
        functools.partial(gram_kernel, width // QBLOCK),
        out_shape=jax.ShapeDtypeStruct((PANEL, width), F32),
        grid_spec=pltpu.PrefetchScalarGridSpec(
            num_scalar_prefetch=1,
            grid=(tokens // step,),
            in_specs=[
                pl.BlockSpec((step, width), lambda k, place: (k, place[0])),
                pl.BlockSpec((step, QBLOCK), lambda k, place: (k, 0)),
                pl.BlockSpec((PANEL, step), lambda k, place: (0, k)),
            ],
            out_specs=pl.BlockSpec((PANEL, width), lambda k, place: (0, 0)),
            scratch_shapes=[pltpu.VMEM((step, width), BF16)],
        ),
        compiler_params=pltpu.CompilerParams(vmem_limit_bytes=40 << 20),
        cost_estimate=pl.CostEstimate(
            flops=2 * tokens * width * PANEL,
            bytes_accessed=2 * tokens * width + 4 * PANEL * width,
            transcendentals=0,
        ),
    )(col.reshape(1).astype(jnp.int32), quantized, scale_pad, panel_t)


def inverse_kernel(head_ref, out_ref, pair_ref):
    size = PANEL
    rows = lax.broadcasted_iota(jnp.int32, (size, size), 0)
    cols = lax.broadcasted_iota(jnp.int32, (size, size), 1)
    eye = jnp.where(rows == cols, 1.0, 0.0).astype(F32)
    head = head_ref[...]
    damping = 0.01 * (jnp.sum(head * eye) / size)
    block = head + damping * eye
    high = jnp.max(jnp.sum(jnp.abs(block), axis=0))
    start = 2.0 / (high + damping)
    spread = (high - damping) / (high + damping)
    pair_ref[:size] = start * eye
    pair_ref[size:] = start * block

    def more(spread):
        return spread > 1e-3

    def step(spread):
        square = spread * spread
        gain = 2.0 / (2.0 - square)
        turn = gain * (2.0 * eye - pair_ref[size:])
        pair_ref[...] = dot_high(pair_ref[...], turn)
        return square / (2.0 - square)

    lax.while_loop(more, step, spread)
    out = pair_ref[:size]
    for _ in range(2):
        out = out + dot_high(out, eye - dot_high(block, out))
    out_ref[...] = out


def invert(head):
    return pl.pallas_call(
        inverse_kernel,
        out_shape=jax.ShapeDtypeStruct((PANEL, PANEL), F32),
        scratch_shapes=[pltpu.VMEM((2 * PANEL, PANEL), F32)],
        compiler_params=pltpu.CompilerParams(vmem_limit_bytes=32 << 20),
        cost_estimate=pl.CostEstimate(
            flops=28 * 12 * PANEL**3, bytes_accessed=8 * PANEL * PANEL, transcendentals=0
        ),
    )(head)


def gains_kernel(inverse_ref, first_ref, second_ref, third_ref, high_ref, low_ref):
    total = first_ref[...] + second_ref[...] + third_ref[...]
    gains = dot_high(inverse_ref[...], total)
    high = gains.astype(BF16)
    high_ref[...] = high
    low_ref[...] = (gains - high.astype(F32)).astype(BF16)


def make_gains(inverse, parts):
    width = parts[0].shape[1]
    shape = jax.ShapeDtypeStruct((PANEL, width), BF16)
    return pl.pallas_call(
        gains_kernel,
        out_shape=(shape, shape),
        compiler_params=pltpu.CompilerParams(vmem_limit_bytes=32 << 20),
        cost_estimate=pl.CostEstimate(
            flops=12 * PANEL * PANEL * width, bytes_accessed=16 * PANEL * width, transcendentals=0
        ),
    )(inverse, *parts)


def update_kernel(count, aliased, place_ref, weights_ref, error_ref, *refs):
    gains = refs[:count]
    out_ref = refs[-1]
    error = error_ref[...]
    total = weights_ref[...].astype(F32)
    for gain in gains:
        total = total + jnp.dot(error, gain[...], preferred_element_type=F32)
    out_ref[...] = total.astype(BF16)

    @pl.when(place_ref[1] == 1)
    def _():
        out_ref[:, :PANEL] = weights_ref[:, :PANEL] - error


def update_block(out, weights, error, gains, col, first):
    rows, cols = weights.shape
    width = gains[0].shape[1]
    if width % QBLOCK or width < PANEL:
        start = col * width
        total = lax.dynamic_slice_in_dim(weights, start, width, 1).astype(F32)
        for gain in gains:
            total = total + jnp.dot(error, gain, preferred_element_type=F32)
        if out is None:
            out = jnp.zeros_like(weights)
        return lax.dynamic_update_slice_in_dim(out, total.astype(BF16), start, 1)
    step = min(rows, 256)
    place = jnp.stack([col, (first & (col == 0)).astype(jnp.int32)]).astype(jnp.int32)
    specs = [
        pl.BlockSpec((step, width), lambda i, place: (i, place[0])),
        pl.BlockSpec((step, PANEL), lambda i, place: (i, 0)),
    ] + [pl.BlockSpec((PANEL, width), lambda i, place: (0, 0))] * len(gains)
    args = [place, weights, error, *gains]
    aliases = {}
    if out is not None:
        specs.append(pl.BlockSpec(memory_space=pl.ANY))
        aliases = {len(args): 0}
        args.append(out)
    return pl.pallas_call(
        functools.partial(update_kernel, len(gains), out is not None),
        out_shape=jax.ShapeDtypeStruct((rows, cols), BF16),
        grid_spec=pltpu.PrefetchScalarGridSpec(
            num_scalar_prefetch=1,
            grid=(rows // step,),
            in_specs=specs,
            out_specs=pl.BlockSpec((step, width), lambda i, place: (i, place[0])),
        ),
        input_output_aliases=aliases,
        compiler_params=pltpu.CompilerParams(vmem_limit_bytes=32 << 20),
        cost_estimate=pl.CostEstimate(
            flops=2 * rows * width * PANEL * len(gains),
            bytes_accessed=4 * rows * width,
            transcendentals=0,
        ),
    )(*args)


def swap(x, axis, bit):
    size = lax.axis_size(axis)
    return lax.ppermute(x, axis, [(i, i ^ bit) for i in range(size)])


def from_first(x, axis):
    size = lax.axis_size(axis)
    index = lax.axis_index(axis)
    held, result = x, x
    for hop in range(size - 1):
        held = lax.ppermute(held, axis, [(hop, hop + 1)])
        result = jnp.where(index == hop + 1, held, result)
    return result


def shards(quantized, exponents, weights, keep_mask):
    tokens, cols = quantized.shape
    toks, rows = lax.axis_size("tok"), lax.axis_size("row")
    tok, row, feat = lax.axis_index("tok"), lax.axis_index("row"), lax.axis_index("feat")
    width = cols // (toks * rows)

    share = tokens // rows
    scale = jnp.exp2(exponents.astype(F32))
    scale_pad = jnp.pad(scale, ((0, 0), (0, -scale.shape[1] % QBLOCK)))
    piece = share // CHUNKS
    own, other = [], []
    for c in range(CHUNKS):
        at = row * share + c * piece
        raw = lax.dynamic_slice(quantized, (at, 0), (piece, PANEL))
        exps = lax.dynamic_slice(scale, (at, 0), (piece, PANEL // QBLOCK)).astype(BF16)
        acts = (raw.reshape(piece, PANEL // QBLOCK, QBLOCK) * exps[:, :, None]).reshape(piece, PANEL)
        mine = from_first(acts.T, "feat")
        own.append(mine)
        other.append(swap(mine, "row", 1))
    mine, theirs = jnp.concatenate(own, axis=1), jnp.concatenate(other, axis=1)
    panel_t = jnp.concatenate(
        [jnp.where(row == 0, mine, theirs), jnp.where(row == 0, theirs, mine)], axis=1
    )

    error = from_first(
        jnp.where(keep_mask == 0, weights[:, :PANEL], jnp.zeros((), BF16)), "feat"
    )

    head = lax.dot_general(
        panel_t, panel_t, (((1,), (1,)), ((), ())), preferred_element_type=F32
    )
    head = head + swap(head, "tok", 1)
    head = head + swap(head, "tok", 2)

    def gram(k):
        return gram_block(quantized, scale_pad, panel_t, row * toks + (tok ^ k), width)

    block3 = gram(3)
    from3 = swap(block3, "tok", 1)
    block2 = gram(2)
    fromx = swap(block2 + from3, "tok", 2)
    block1 = gram(1)
    from1 = swap(block1, "tok", 1)
    block0 = gram(0)
    inverse = invert(head)
    high, low = make_gains(inverse, (block0, from1, fromx))

    half = PANEL // 2
    near_high, near_low = swap(high, "tok", 1), swap(low, "tok", 1)
    in_x, in_y = swap(high, "tok", 2), swap(high, "row", 1)
    far = jnp.concatenate([swap(in_y[:half], "tok", 2), swap(in_x[half:], "row", 1)], axis=0)
    near_x, near_y, near_far = swap(in_x, "tok", 1), swap(in_y, "tok", 1), swap(far, "tok", 1)

    out = None
    plan = [
        ((high, low), 0, 0),
        ((near_high, near_low), 1, 0),
        ((in_x,), 2, 0),
        ((in_y,), 0, 1),
        ((near_x,), 3, 0),
        ((near_y,), 1, 1),
        ((far,), 2, 1),
        ((near_far,), 3, 1),
    ]
    for gains, tok_bits, row_bit in plan:
        col = (row ^ row_bit) * toks + (tok ^ tok_bits)
        out = update_block(out, weights, error, gains, col, feat == 0)
    if width % QBLOCK or width < PANEL:
        panel = jnp.where(feat == 0, weights[:, :PANEL] - error, out[:, :PANEL])
        out = lax.dynamic_update_slice_in_dim(out, panel, 0, 1)
    return out


def solution(mesh):
    placed = (
        P("tok", "feat"),
        P("tok", "feat"),
        P(("tok", "row"), "feat"),
        P(("tok", "row"), None),
    )
    return jax.shard_map(
        shards, mesh=mesh, in_specs=placed, out_specs=P(("tok", "row"), "feat"), check_vma=False
    )
```

```python
import functools

import jax
import jax.numpy as jnp
from jax import lax
from jax.experimental import pallas as pl
from jax.experimental.pallas import tpu as pltpu
from jax.sharding import PartitionSpec as P

PANEL = 256
QBLOCK = 128
ROUNDS = 4
F32 = jnp.float32
BF16 = jnp.bfloat16
MIB = 1 << 20


def dot_high(left, right):
    return jnp.dot(left, right, precision=lax.Precision.HIGHEST, preferred_element_type=F32)


def panel_kernel(place_ref, quant_ref, exps_ref, first_ref, second_ref):
    scale = jnp.exp2(exps_ref[:, : PANEL // QBLOCK].astype(F32))
    rows = scale.shape[0]
    wide = [
        jnp.broadcast_to(scale[:, c : c + 1], (rows, QBLOCK)) for c in range(PANEL // QBLOCK)
    ]
    acts = quant_ref[...].astype(F32) * jnp.concatenate(wide, axis=1)
    turned = acts.T.astype(BF16)
    half = rows // 2
    first_ref[...] = turned[:, :half]
    second_ref[...] = turned[:, half:]


def panel_piece(quantized, exponents, at, piece):
    blocks = exponents.shape[1]
    shape = jax.ShapeDtypeStruct((PANEL, piece // 2), BF16)
    return pl.pallas_call(
        panel_kernel,
        out_shape=(shape, shape),
        grid_spec=pltpu.PrefetchScalarGridSpec(
            num_scalar_prefetch=1,
            grid=(1,),
            in_specs=[
                pl.BlockSpec((piece, PANEL), lambda i, place: (place[0], 0)),
                pl.BlockSpec((piece, blocks), lambda i, place: (place[0], 0)),
            ],
            out_specs=[pl.BlockSpec((PANEL, piece // 2), lambda i, place: (0, 0))] * 2,
        ),
        compiler_params=pltpu.CompilerParams(vmem_limit_bytes=48 * MIB),
        cost_estimate=pl.CostEstimate(
            flops=piece * PANEL, bytes_accessed=4 * piece * PANEL, transcendentals=0
        ),
    )(at.reshape(1).astype(jnp.int32), quantized, exponents)


def head_kernel(place_ref, panel_ref, out_ref):
    @pl.when(pl.program_id(0) == 0)
    def _():
        out_ref[...] = jnp.zeros_like(out_ref)

    panel = panel_ref[...]
    out_ref[...] += lax.dot_general(
        panel, panel, (((1,), (1,)), ((), ())), preferred_element_type=F32
    )


def slot(step, start, slots):
    return jnp.where(step < ROUNDS, start + step, slots // 2 + start + step - ROUNDS)


def head_block(stack, start):
    slots, _, piece = stack.shape
    return pl.pallas_call(
        head_kernel,
        out_shape=jax.ShapeDtypeStruct((PANEL, PANEL), F32),
        grid_spec=pltpu.PrefetchScalarGridSpec(
            num_scalar_prefetch=1,
            grid=(2 * ROUNDS,),
            in_specs=[
                pl.BlockSpec(
                    (None, PANEL, piece), lambda k, place: (slot(k, place[0], slots), 0, 0)
                )
            ],
            out_specs=pl.BlockSpec((PANEL, PANEL), lambda k, place: (0, 0)),
        ),
        compiler_params=pltpu.CompilerParams(vmem_limit_bytes=32 * MIB),
        cost_estimate=pl.CostEstimate(
            flops=4 * ROUNDS * piece * PANEL * PANEL,
            bytes_accessed=4 * ROUNDS * piece * PANEL,
            transcendentals=0,
        ),
    )(start.reshape(1).astype(jnp.int32), stack)


def gram_kernel(blocks, place_ref, quant_ref, rows_ref, left_ref, right_ref, *refs):
    out_ref = refs[-1]

    @pl.when(pl.program_id(0) == 0)
    def _():
        out_ref[...] = refs[0][...] if len(refs) > 1 else jnp.zeros_like(out_ref)

    rows = rows_ref[...]
    turned = rows.T
    step = quant_ref.shape[0]
    panel = jnp.concatenate([left_ref[...], right_ref[...]], axis=1)
    for c in range(0, blocks, 2):
        left = panel * jnp.broadcast_to(rows[c : c + 1].astype(BF16), (PANEL, step))
        right = quant_ref[:, c * QBLOCK : (c + 1) * QBLOCK]
        if c + 1 < blocks:
            ratio = jnp.broadcast_to(turned[:, c + 1 : c + 2], (step, QBLOCK)).astype(BF16)
            second = quant_ref[:, (c + 1) * QBLOCK : (c + 2) * QBLOCK] * ratio
            right = jnp.concatenate([right, second], axis=1)
        span = slice(c * QBLOCK, c * QBLOCK + right.shape[1])
        out_ref[:, span] += jnp.dot(left, right, preferred_element_type=F32)


def gram_block(quantized, exponents, scale_rows, stack, row, start, col, width, extra=None):
    tokens, _ = quantized.shape
    slots, _, piece = stack.shape
    blocks = width // QBLOCK
    if scale_rows is None:
        half = slots // 2
        held = [lax.dynamic_slice_in_dim(stack, start + i * half, ROUNDS, 0) for i in range(2)]
        panel = jnp.concatenate(held, axis=0).transpose(1, 0, 2).reshape(PANEL, tokens)
        quant = lax.dynamic_slice_in_dim(quantized, col * width, width, 1)
        scale = jnp.exp2(exponents.astype(F32)).astype(BF16)
        acts = quant * jnp.take(scale, (col * width + jnp.arange(width)) // QBLOCK, axis=1)
        acts = jnp.roll(acts, -row * (tokens // 2), axis=0)
        total = jnp.dot(panel, acts, preferred_element_type=F32)
        return total if extra is None else total + extra
    step = 2 * piece
    steps = tokens // step
    place = jnp.stack([row, start, col]).astype(jnp.int32)

    def tokens_at(k, place):
        return lax.rem(k + place[0] * (steps // 2), steps)

    specs = [
        pl.BlockSpec((step, width), lambda k, place: (tokens_at(k, place), place[2])),
        pl.BlockSpec((8, step), lambda k, place: (place[2], tokens_at(k, place))),
        pl.BlockSpec((None, PANEL, piece), lambda k, place: (slot(2 * k, place[1], slots), 0, 0)),
        pl.BlockSpec(
            (None, PANEL, piece), lambda k, place: (slot(2 * k + 1, place[1], slots), 0, 0)
        ),
    ]
    args = [place, quantized, scale_rows, stack, stack]
    if extra is not None:
        specs.append(pl.BlockSpec((PANEL, width), lambda k, place: (0, 0)))
        args.append(extra)
    return pl.pallas_call(
        functools.partial(gram_kernel, blocks),
        out_shape=jax.ShapeDtypeStruct((PANEL, width), F32),
        grid_spec=pltpu.PrefetchScalarGridSpec(
            num_scalar_prefetch=1,
            grid=(steps,),
            in_specs=specs,
            out_specs=pl.BlockSpec((PANEL, width), lambda k, place: (0, 0)),
        ),
        compiler_params=pltpu.CompilerParams(vmem_limit_bytes=32 * MIB),
        cost_estimate=pl.CostEstimate(
            flops=2 * tokens * width * PANEL,
            bytes_accessed=2 * tokens * width + 4 * PANEL * width,
            transcendentals=0,
        ),
    )(*args)


def inverse_kernel(head_ref, out_ref, pair_ref):
    size = PANEL
    rows = lax.broadcasted_iota(jnp.int32, (size, size), 0)
    cols = lax.broadcasted_iota(jnp.int32, (size, size), 1)
    eye = jnp.where(rows == cols, 1.0, 0.0).astype(F32)
    head = head_ref[...]
    damping = 0.01 * (jnp.sum(head * eye) / size)
    block = head + damping * eye
    high = jnp.max(jnp.sum(jnp.abs(block), axis=0))
    start = 2.0 / (high + damping)
    spread = (high - damping) / (high + damping)
    pair_ref[:size] = start * eye
    pair_ref[size:] = start * block

    def more(spread):
        return spread > 1e-3

    def step(spread):
        square = spread * spread
        gain = 2.0 / (2.0 - square)
        turn = gain * (2.0 * eye - pair_ref[size:])
        pair_ref[...] = dot_high(pair_ref[...], turn)
        return square / (2.0 - square)

    lax.while_loop(more, step, spread)
    out = pair_ref[:size]
    for _ in range(2):
        out = out + dot_high(out, eye - dot_high(block, out))
    out_ref[...] = out


def invert(head):
    return pl.pallas_call(
        inverse_kernel,
        out_shape=jax.ShapeDtypeStruct((PANEL, PANEL), F32),
        scratch_shapes=[pltpu.VMEM((2 * PANEL, PANEL), F32)],
        compiler_params=pltpu.CompilerParams(vmem_limit_bytes=32 * MIB),
        cost_estimate=pl.CostEstimate(
            flops=28 * 12 * PANEL**3, bytes_accessed=8 * PANEL * PANEL, transcendentals=0
        ),
    )(head)


def gains_kernel(inverse_ref, first_ref, second_ref, third_ref, high_ref, pair_ref):
    total = first_ref[...] + second_ref[...] + third_ref[...]
    gains = dot_high(inverse_ref[...], total)
    high = gains.astype(BF16)
    high_ref[...] = high
    pair_ref[:PANEL] = high
    pair_ref[PANEL:] = (gains - high.astype(F32)).astype(BF16)


def make_gains(inverse, parts):
    width = parts[0].shape[1]
    return pl.pallas_call(
        gains_kernel,
        out_shape=(
            jax.ShapeDtypeStruct((PANEL, width), BF16),
            jax.ShapeDtypeStruct((2 * PANEL, width), BF16),
        ),
        compiler_params=pltpu.CompilerParams(vmem_limit_bytes=32 * MIB),
        cost_estimate=pl.CostEstimate(
            flops=12 * PANEL * PANEL * width, bytes_accessed=16 * PANEL * width, transcendentals=0
        ),
    )(inverse, *parts)


def update_kernel(count, place_ref, weights_ref, error_ref, *refs):
    gains, out_ref = refs[:count], refs[-1]
    for j in range(count):

        @pl.when(pl.program_id(0) == j)
        def _():
            total = weights_ref[...].astype(F32)
            for at in range(0, gains[j].shape[0], PANEL):
                total += jnp.dot(
                    error_ref[...], gains[j][at : at + PANEL], preferred_element_type=F32
                )
            out_ref[...] = total.astype(BF16)

    @pl.when(place_ref[count + pl.program_id(0)] == 1)
    def _():
        out_ref[:, :PANEL] = weights_ref[:, :PANEL] - error_ref[...]


def update_blocks(out, weights, error, gains, spots, first):
    rows, cols = weights.shape
    width = gains[0].shape[1]
    count = len(gains)
    if width % QBLOCK or width < PANEL:
        out = jnp.zeros_like(weights) if out is None else out
        for gain, col in zip(gains, spots):
            total = lax.dynamic_slice_in_dim(weights, col * width, width, 1).astype(F32)
            for at in range(0, gain.shape[0], PANEL):
                total += jnp.dot(error, gain[at : at + PANEL], preferred_element_type=F32)
            out = lax.dynamic_update_slice_in_dim(out, total.astype(BF16), col * width, 1)
        return out
    step = min(rows, 512)
    place = jnp.stack(list(spots) + [first & (col == 0) for col in spots]).astype(jnp.int32)
    specs = [
        pl.BlockSpec((step, width), lambda j, i, place: (i, place[j])),
        pl.BlockSpec((step, PANEL), lambda j, i, place: (i, 0)),
    ] + [pl.BlockSpec(gain.shape, lambda j, i, place: (0, 0)) for gain in gains]
    args = [place, weights, error, *gains]
    aliases = {}
    if out is not None:
        specs.append(pl.BlockSpec(memory_space=pl.ANY))
        aliases = {len(args): 0}
        args.append(out)
    return pl.pallas_call(
        functools.partial(update_kernel, count),
        out_shape=jax.ShapeDtypeStruct((rows, cols), BF16),
        grid_spec=pltpu.PrefetchScalarGridSpec(
            num_scalar_prefetch=1,
            grid=(count, rows // step),
            in_specs=specs,
            out_specs=pl.BlockSpec((step, width), lambda j, i, place: (i, place[j])),
        ),
        input_output_aliases=aliases,
        compiler_params=pltpu.CompilerParams(vmem_limit_bytes=56 * MIB),
        cost_estimate=pl.CostEstimate(
            flops=2 * rows * width * PANEL * count,
            bytes_accessed=4 * rows * width * count,
            transcendentals=0,
        ),
    )(*args)


def swap(x, axis, bit):
    size = lax.axis_size(axis)
    return lax.ppermute(x, axis, [(i, i ^ bit) for i in range(size)])


def forward(x, axis):
    size = lax.axis_size(axis)
    return lax.ppermute(x, axis, [(i, i + 1) for i in range(size - 1)])


def shards(quantized, exponents, weights, keep_mask):
    tokens, cols = quantized.shape
    toks, rows, feats = lax.axis_size("tok"), lax.axis_size("row"), lax.axis_size("feat")
    tok, row, feat = lax.axis_index("tok"), lax.axis_index("row"), lax.axis_index("feat")
    width = cols // (toks * rows)
    root = feat == 0

    piece = tokens // rows // ROUNDS
    sources = [
        panel_piece(quantized, exponents, row * ROUNDS + c, piece) for c in range(ROUNDS)
    ]
    none = jnp.zeros((PANEL, piece // 2), BF16)
    held = [jnp.where(root, x, none) for x in sources[0]]
    own, other = [], []
    for r in range(ROUNDS + feats - 1):
        both = jnp.concatenate(held, axis=1)
        own.append(both)
        other.append(swap(both, "row", 1))
        if r < ROUNDS + feats - 2:
            held = [forward(x, "feat") for x in held]
            if r + 1 < ROUNDS:
                held = [jnp.where(root, x, y) for x, y in zip(sources[r + 1], held)]
    stack = jnp.stack(own + other)

    scale_rows = None
    if width % QBLOCK == 0 and width // QBLOCK <= 8:
        blocks = width // QBLOCK
        exps = exponents.T.reshape(toks * rows, blocks, tokens)
        before = jnp.pad(exps[:, :-1], ((0, 0), (1, 0), (0, 0)))
        odd = (jnp.arange(blocks) % 2 == 1)[None, :, None]
        exps = jnp.where(odd, exps - before, exps)
        exps = jnp.pad(exps, ((0, 0), (0, 8 - blocks), (0, 0)))
        scale_rows = jnp.exp2(exps.astype(F32)).reshape(-1, tokens)

    error = jnp.where(keep_mask == 0, weights[:, :PANEL], jnp.zeros((), BF16))
    error, stack = lax.optimization_barrier((error, stack))
    errors = [error, forward(error, "feat")]

    def gram(k, extra=None):
        col = row * toks + (tok ^ k)
        return gram_block(
            quantized, exponents, scale_rows, stack, row, feat, col, width, extra
        )

    head = head_block(stack, feat)
    from_core = swap(head, "tok", 1)
    from3 = swap(gram(3), "tok", 1)
    head = head + from_core
    head = head + swap(head, "tok", 2)
    block2 = gram(2, from3)
    fromx = swap(block2, "tok", 2)
    from1 = swap(gram(1), "tok", 1)
    block0 = gram(0)
    inverse = invert(head)
    for _ in range(feats - 2):
        if len(errors) == 2:
            block0, last = lax.optimization_barrier((block0, errors[-1]))
        elif len(errors) == 3:
            inverse, last = lax.optimization_barrier((inverse, errors[-1]))
        else:
            last = errors[-1]
        errors[-1] = last
        errors.append(forward(last, "feat"))
    for hop in range(1, feats):
        error = jnp.where(feat == hop, errors[hop], error)
    high, pair = make_gains(inverse, (block0, from1, fromx))

    half = PANEL // 2
    in_x, in_y = swap(high, "tok", 2), swap(high, "row", 1)
    near = swap(pair, "tok", 1)
    far = jnp.concatenate([swap(in_y[:half], "tok", 2), swap(in_x[half:], "row", 1)], axis=0)
    near_x, near_y, near_far = swap(in_x, "tok", 1), swap(in_y, "tok", 1), swap(far, "tok", 1)

    out = None
    plan = [
        [(pair, 0, 0), (near, 1, 0)],
        [(in_x, 2, 0), (in_y, 0, 1), (near_x, 3, 0), (near_y, 1, 1)],
        [(far, 2, 1), (near_far, 3, 1)],
    ]
    for group in plan:
        spots = [(row ^ row_bit) * toks + (tok ^ tok_bits) for _, tok_bits, row_bit in group]
        out = update_blocks(out, weights, error, [gain for gain, _, _ in group], spots, root)
    if width % QBLOCK or width < PANEL:
        panel = jnp.where(root, weights[:, :PANEL] - error, out[:, :PANEL])
        out = lax.dynamic_update_slice_in_dim(out, panel, 0, 1)
    return out


def solution(mesh):
    placed = (
        P("tok", "feat"),
        P("tok", "feat"),
        P(("tok", "row"), "feat"),
        P(("tok", "row"), None),
    )
    return jax.shard_map(
        shards, mesh=mesh, in_specs=placed, out_specs=P(("tok", "row"), "feat"), check_vma=False
    )
```

```python
import functools

import jax
import jax.numpy as jnp
from jax import lax
from jax.experimental import pallas as pl
from jax.experimental.pallas import tpu as pltpu
from jax.sharding import PartitionSpec as P

PANEL = 256
QBLOCK = 128
ROUNDS = 4
SPLIT = 4
F32 = jnp.float32
BF16 = jnp.bfloat16
MIB = 1 << 20


def dot_high(left, right):
    return jnp.dot(left, right, precision=lax.Precision.HIGHEST, preferred_element_type=F32)


def panel_kernel(place_ref, quant_ref, exps_ref, out_ref):
    scale = jnp.exp2(exps_ref[:, : PANEL // QBLOCK].astype(F32))
    rows = scale.shape[0]
    wide = [
        jnp.broadcast_to(scale[:, c : c + 1], (rows, QBLOCK)) for c in range(PANEL // QBLOCK)
    ]
    acts = quant_ref[...].astype(F32) * jnp.concatenate(wide, axis=1)
    out_ref[...] = acts.T.astype(BF16)


def panel_piece(quantized, exponents, at, piece):
    blocks = exponents.shape[1]
    return pl.pallas_call(
        panel_kernel,
        out_shape=jax.ShapeDtypeStruct((PANEL, piece), BF16),
        grid_spec=pltpu.PrefetchScalarGridSpec(
            num_scalar_prefetch=1,
            grid=(1,),
            in_specs=[
                pl.BlockSpec((piece, PANEL), lambda i, place: (place[0], 0)),
                pl.BlockSpec((piece, blocks), lambda i, place: (place[0], 0)),
            ],
            out_specs=pl.BlockSpec((PANEL, piece), lambda i, place: (0, 0)),
        ),
        compiler_params=pltpu.CompilerParams(vmem_limit_bytes=48 * MIB),
        cost_estimate=pl.CostEstimate(
            flops=piece * PANEL, bytes_accessed=4 * piece * PANEL, transcendentals=0
        ),
    )(at.reshape(1).astype(jnp.int32), quantized, exponents)


def head_kernel(place_ref, panel_ref, out_ref):
    @pl.when(pl.program_id(0) == 0)
    def _():
        out_ref[...] = jnp.zeros_like(out_ref)

    panel = panel_ref[...]
    out_ref[...] += lax.dot_general(
        panel, panel, (((1,), (1,)), ((), ())), preferred_element_type=F32
    )


def slot(step, start, slots):
    return jnp.where(step < ROUNDS, start + step, slots // 2 + start + step - ROUNDS)


def head_block(stack, start):
    slots, _, piece = stack.shape
    return pl.pallas_call(
        head_kernel,
        out_shape=jax.ShapeDtypeStruct((PANEL, PANEL), F32),
        grid_spec=pltpu.PrefetchScalarGridSpec(
            num_scalar_prefetch=1,
            grid=(2 * ROUNDS,),
            in_specs=[
                pl.BlockSpec(
                    (None, PANEL, piece), lambda k, place: (slot(k, place[0], slots), 0, 0)
                )
            ],
            out_specs=pl.BlockSpec((PANEL, PANEL), lambda k, place: (0, 0)),
        ),
        compiler_params=pltpu.CompilerParams(vmem_limit_bytes=32 * MIB),
        cost_estimate=pl.CostEstimate(
            flops=4 * ROUNDS * piece * PANEL * PANEL,
            bytes_accessed=4 * ROUNDS * piece * PANEL,
            transcendentals=0,
        ),
    )(start.reshape(1).astype(jnp.int32), stack)


def gram_kernel(blocks, place_ref, rows_ref, left_ref, right_ref, *refs):
    quants, refs, out_ref = refs[:SPLIT], refs[SPLIT:], refs[-1]

    @pl.when(pl.program_id(0) == 0)
    def _():
        out_ref[...] = refs[0][...] if len(refs) > 1 else jnp.zeros_like(out_ref)

    rows = rows_ref[...]
    turned = rows.T
    step = rows.shape[1]

    def quant(c):
        return jnp.concatenate([q[:, c * QBLOCK : (c + 1) * QBLOCK] for q in quants], axis=0)

    panel = jnp.concatenate([left_ref[...], right_ref[...]], axis=1)
    for c in range(0, blocks, 2):
        left = panel * jnp.broadcast_to(rows[c : c + 1].astype(BF16), (PANEL, step))
        right = quant(c)
        if c + 1 < blocks:
            ratio = jnp.broadcast_to(turned[:, c + 1 : c + 2], (step, QBLOCK)).astype(BF16)
            right = jnp.concatenate([right, quant(c + 1) * ratio], axis=1)
        span = slice(c * QBLOCK, c * QBLOCK + right.shape[1])
        out_ref[:, span] += jnp.dot(left, right, preferred_element_type=F32)


def gram_block(quantized, exponents, scale_rows, stack, row, start, col, width, extra=None):
    tokens, _ = quantized.shape
    slots, _, piece = stack.shape
    blocks = width // QBLOCK
    if scale_rows is None:
        half = slots // 2
        held = [lax.dynamic_slice_in_dim(stack, start + i * half, ROUNDS, 0) for i in range(2)]
        panel = jnp.concatenate(held, axis=0).transpose(1, 0, 2).reshape(PANEL, tokens)
        quant = lax.dynamic_slice_in_dim(quantized, col * width, width, 1)
        scale = jnp.exp2(exponents.astype(F32)).astype(BF16)
        acts = quant * jnp.take(scale, (col * width + jnp.arange(width)) // QBLOCK, axis=1)
        acts = jnp.roll(acts, -row * (tokens // 2), axis=0)
        total = jnp.dot(panel, acts, preferred_element_type=F32)
        return total if extra is None else total + extra
    step = 2 * piece
    steps = tokens // step
    place = jnp.stack([row, start, col]).astype(jnp.int32)

    def tokens_at(k, place):
        return lax.rem(k + place[0] * (steps // 2), steps)

    specs = [
        pl.BlockSpec((8, step), lambda k, place: (place[2], tokens_at(k, place))),
        pl.BlockSpec((None, PANEL, piece), lambda k, place: (slot(2 * k, place[1], slots), 0, 0)),
        pl.BlockSpec(
            (None, PANEL, piece), lambda k, place: (slot(2 * k + 1, place[1], slots), 0, 0)
        ),
    ]
    specs += [
        pl.BlockSpec(
            (step // SPLIT, width),
            functools.partial(
                lambda i, k, place: (SPLIT * tokens_at(k, place) + i, place[2]), i
            ),
        )
        for i in range(SPLIT)
    ]
    args = [place, scale_rows, stack, stack] + [quantized] * SPLIT
    if extra is not None:
        specs.append(pl.BlockSpec((PANEL, width), lambda k, place: (0, 0)))
        args.append(extra)
    return pl.pallas_call(
        functools.partial(gram_kernel, blocks),
        out_shape=jax.ShapeDtypeStruct((PANEL, width), F32),
        grid_spec=pltpu.PrefetchScalarGridSpec(
            num_scalar_prefetch=1,
            grid=(steps,),
            in_specs=specs,
            out_specs=pl.BlockSpec((PANEL, width), lambda k, place: (0, 0)),
        ),
        compiler_params=pltpu.CompilerParams(vmem_limit_bytes=32 * MIB),
        cost_estimate=pl.CostEstimate(
            flops=2 * tokens * width * PANEL,
            bytes_accessed=2 * tokens * width + 4 * PANEL * width,
            transcendentals=0,
        ),
    )(*args)


def inverse_kernel(head_ref, out_ref, pair_ref):
    size = PANEL
    rows = lax.broadcasted_iota(jnp.int32, (size, size), 0)
    cols = lax.broadcasted_iota(jnp.int32, (size, size), 1)
    eye = jnp.where(rows == cols, 1.0, 0.0).astype(F32)
    head = head_ref[...]
    damping = 0.01 * (jnp.sum(head * eye) / size)
    block = head + damping * eye
    high = jnp.max(jnp.sum(jnp.abs(block), axis=0))
    start = 2.0 / (high + damping)
    spread = (high - damping) / (high + damping)
    pair_ref[:size] = start * eye
    pair_ref[size:] = start * block

    def more(spread):
        return spread > 1e-3

    def step(spread):
        square = spread * spread
        gain = 2.0 / (2.0 - square)
        turn = gain * (2.0 * eye - pair_ref[size:])
        pair_ref[...] = dot_high(pair_ref[...], turn)
        return square / (2.0 - square)

    lax.while_loop(more, step, spread)
    out = pair_ref[:size]
    for _ in range(2):
        out = out + dot_high(out, eye - dot_high(block, out))
    out_ref[...] = out


def invert(head):
    return pl.pallas_call(
        inverse_kernel,
        out_shape=jax.ShapeDtypeStruct((PANEL, PANEL), F32),
        scratch_shapes=[pltpu.VMEM((2 * PANEL, PANEL), F32)],
        compiler_params=pltpu.CompilerParams(vmem_limit_bytes=32 * MIB),
        cost_estimate=pl.CostEstimate(
            flops=28 * 12 * PANEL**3, bytes_accessed=8 * PANEL * PANEL, transcendentals=0
        ),
    )(head)


def gains_kernel(inverse_ref, first_ref, second_ref, third_ref, high_ref, pair_ref):
    total = first_ref[...] + second_ref[...] + third_ref[...]
    gains = dot_high(inverse_ref[...], total)
    high = gains.astype(BF16)
    high_ref[...] = high
    pair_ref[:PANEL] = high
    pair_ref[PANEL:] = (gains - high.astype(F32)).astype(BF16)


def make_gains(inverse, parts):
    width = parts[0].shape[1]
    return pl.pallas_call(
        gains_kernel,
        out_shape=(
            jax.ShapeDtypeStruct((PANEL, width), BF16),
            jax.ShapeDtypeStruct((2 * PANEL, width), BF16),
        ),
        compiler_params=pltpu.CompilerParams(vmem_limit_bytes=32 * MIB),
        cost_estimate=pl.CostEstimate(
            flops=12 * PANEL * PANEL * width, bytes_accessed=16 * PANEL * width, transcendentals=0
        ),
    )(inverse, *parts)


def update_kernel(shapes, place_ref, error_ref, weights_ref, *refs):
    count = len(shapes)
    groups, at = [], 0
    for pieces in shapes:
        groups.append(refs[at : at + len(pieces)])
        at += len(pieces)
    out_ref, read_ref, made_ref, read_sems, made_sems = refs[-5:]
    _, parts, step, width = read_ref.shape

    def window(ref, j, i):
        col = pl.multiple_of(place_ref[j] * width, QBLOCK)
        return ref.at[pl.ds(i * step, step), pl.ds(col, width)]

    def read(j, i):
        return pltpu.make_async_copy(window(weights_ref, j, i), read_ref.at[j, i], read_sems.at[j, i])

    def made(j, i):
        return pltpu.make_async_copy(made_ref.at[j, i], window(out_ref, j, i), made_sems.at[j, i])

    spots = [(j, i) for j in range(count) for i in range(parts)]
    for j, i in spots:
        read(j, i).start()
    for j, i in spots:
        read(j, i).wait()
        error = error_ref[i * step : (i + 1) * step, :]
        total = read_ref[j, i].astype(F32)
        row = 0
        for gain in groups[j]:
            for top in range(0, gain.shape[0], PANEL):
                size = min(PANEL, gain.shape[0])
                total += jnp.dot(
                    error[:, row : row + size],
                    gain[top : top + size, :],
                    preferred_element_type=F32,
                )
                row = (row + size) % PANEL
        made_ref[j, i] = total.astype(BF16)

        @pl.when(place_ref[count + j] == 1)
        def _():
            made_ref[j, i, :, :PANEL] = read_ref[j, i, :, :PANEL] - error

        made(j, i).start()
    for j, i in spots:
        made(j, i).wait()


def update_blocks(out, weights, error, gains, spots, first):
    rows, cols = weights.shape
    width = gains[0][0].shape[1]
    count = len(gains)
    if width % QBLOCK or width < PANEL:
        out = jnp.zeros_like(weights) if out is None else out
        for pieces, col in zip(gains, spots):
            total = lax.dynamic_slice_in_dim(weights, col * width, width, 1).astype(F32)
            gain = jnp.concatenate(pieces, axis=0)
            for at in range(0, gain.shape[0], PANEL):
                total += jnp.dot(error, gain[at : at + PANEL], preferred_element_type=F32)
            out = lax.dynamic_update_slice_in_dim(out, total.astype(BF16), col * width, 1)
        return out
    parts = 4 if rows % 64 == 0 else 1
    place = jnp.stack(list(spots) + [first & (col == 0) for col in spots]).astype(jnp.int32)
    flat = [piece for pieces in gains for piece in pieces]
    vmem, anywhere = pl.BlockSpec(memory_space=pltpu.VMEM), pl.BlockSpec(memory_space=pl.ANY)
    specs = [pl.BlockSpec(memory_space=pltpu.SMEM), vmem, anywhere] + [vmem] * len(flat)
    args = [place, error, weights, *flat]
    aliases = {}
    if out is not None:
        specs.append(anywhere)
        aliases = {len(args): 0}
        args.append(out)
    buffer = pltpu.VMEM((count, parts, rows // parts, width), BF16)
    sems = pltpu.SemaphoreType.DMA((count, parts))
    return pl.pallas_call(
        functools.partial(update_kernel, [[p.shape for p in pieces] for pieces in gains]),
        out_shape=jax.ShapeDtypeStruct((rows, cols), BF16),
        in_specs=specs,
        out_specs=anywhere,
        scratch_shapes=[buffer, buffer, sems, sems],
        input_output_aliases=aliases,
        compiler_params=pltpu.CompilerParams(vmem_limit_bytes=48 * MIB),
        cost_estimate=pl.CostEstimate(
            flops=2 * rows * width * PANEL * count,
            bytes_accessed=4 * rows * width * count,
            transcendentals=0,
        ),
    )(*args)


def swap(x, axis, bit):
    size = lax.axis_size(axis)
    return lax.ppermute(x, axis, [(i, i ^ bit) for i in range(size)])


def forward(x, axis):
    size = lax.axis_size(axis)
    return lax.ppermute(x, axis, [(i, (i + 1) % size) for i in range(size)])


def shards(quantized, exponents, weights, keep_mask):
    tokens, cols = quantized.shape
    toks, rows, feats = lax.axis_size("tok"), lax.axis_size("row"), lax.axis_size("feat")
    tok, row, feat = lax.axis_index("tok"), lax.axis_index("row"), lax.axis_index("feat")
    width = cols // (toks * rows)
    root = feat == 0

    piece = tokens // rows // ROUNDS
    sources = [
        panel_piece(quantized, exponents, row * ROUNDS + c, piece) for c in range(ROUNDS)
    ]
    error = jnp.where(keep_mask == 0, weights[:, :PANEL], jnp.zeros((), BF16)).T
    extras = -(-error.shape[1] // piece)
    error = jnp.pad(error, ((0, 0), (0, extras * piece - error.shape[1])))
    sources += [error[:, i * piece : (i + 1) * piece] for i in range(extras)]
    held, own, other, late = sources[0], [], [], []
    for r in range(len(sources) + feats - 1):
        if r:
            held = forward(held, "feat")
            if r < len(sources):
                held = jnp.where(root, sources[r], held)
        if r < ROUNDS + feats - 1:
            own.append(held)
            other.append(swap(held, "row", 1))
        if r >= ROUNDS:
            late.append(held)
    stack = jnp.stack(own + other)

    scale_rows = None
    if width % QBLOCK == 0 and width // QBLOCK <= 8:
        blocks = width // QBLOCK
        exps = exponents.T.reshape(toks * rows, blocks, tokens)
        before = jnp.pad(exps[:, :-1], ((0, 0), (1, 0), (0, 0)))
        odd = (jnp.arange(blocks) % 2 == 1)[None, :, None]
        exps = jnp.where(odd, exps - before, exps)
        exps = jnp.pad(exps, ((0, 0), (0, 8 - blocks), (0, 0)))
        scale_rows = jnp.exp2(exps.astype(F32)).reshape(-1, tokens)

    def gram(k, extra=None):
        col = row * toks + (tok ^ k)
        return gram_block(
            quantized, exponents, scale_rows, stack, row, feat, col, width, extra
        )

    head = head_block(stack, feat)
    head = head + swap(head, "tok", 1)
    from3 = swap(gram(3), "tok", 1)
    head = head + swap(head, "tok", 2)
    from1 = swap(gram(1), "tok", 1)
    from3, late[-2] = lax.optimization_barrier((from3, late[-2]))
    block2, head = lax.optimization_barrier((gram(2, from3), head))
    fromx = swap(block2, "tok", 2)
    block0 = gram(0)
    head, late[-1] = lax.optimization_barrier((head, late[-1]))
    inverse = invert(head)
    error = jnp.concatenate(
        list(lax.dynamic_slice_in_dim(jnp.stack(late), feat, extras, 0)), axis=1
    )[:, : weights.shape[0]].T
    inverse, error = lax.optimization_barrier((inverse, error))
    high, pair = make_gains(inverse, (block0, from1, fromx))

    half = PANEL // 2
    in_x, in_y = swap(high, "tok", 2), swap(high, "row", 1)
    near = swap(pair, "tok", 1)
    far = (swap(in_y[:half], "tok", 2), swap(in_x[half:], "row", 1))
    near_x, near_y = swap(in_x, "tok", 1), swap(in_y, "tok", 1)
    near_far = tuple(swap(x, "tok", 1) for x in far)

    out = None
    plan = [
        [((pair,), 0, 0), ((near,), 1, 0)],
        [((in_x,), 2, 0), ((in_y,), 0, 1), ((near_x,), 3, 0), ((near_y,), 1, 1)],
        [(far, 2, 1), (near_far, 3, 1)],
    ]
    for group in plan:
        spots = [(row ^ row_bit) * toks + (tok ^ tok_bits) for _, tok_bits, row_bit in group]
        out = update_blocks(out, weights, error, [gain for gain, _, _ in group], spots, root)
    if width % QBLOCK or width < PANEL:
        panel = jnp.where(root, weights[:, :PANEL] - error, out[:, :PANEL])
        out = lax.dynamic_update_slice_in_dim(out, panel, 0, 1)
    return out


def solution(mesh):
    placed = (
        P("tok", "feat"),
        P("tok", "feat"),
        P(("tok", "row"), "feat"),
        P(("tok", "row"), None),
    )
    return jax.shard_map(
        shards, mesh=mesh, in_specs=placed, out_specs=P(("tok", "row"), "feat"), check_vma=False
    )
```

```python
import functools

import jax
import jax.numpy as jnp
from jax import lax
from jax.experimental import pallas as pl
from jax.experimental.pallas import tpu as pltpu
from jax.sharding import PartitionSpec as P

PANEL = 256
QBLOCK = 128
ROUNDS = 4
F32 = jnp.float32
BF16 = jnp.bfloat16
MIB = 1 << 20


def dot_high(left, right):
    return jnp.dot(left, right, precision=lax.Precision.HIGHEST, preferred_element_type=F32)


def panel_kernel(place_ref, quant_ref, exps_ref, out_ref):
    scale = jnp.exp2(exps_ref[:, : PANEL // QBLOCK].astype(F32))
    rows = scale.shape[0]
    wide = [
        jnp.broadcast_to(scale[:, c : c + 1], (rows, QBLOCK)) for c in range(PANEL // QBLOCK)
    ]
    acts = quant_ref[...].astype(F32) * jnp.concatenate(wide, axis=1)
    out_ref[...] = acts.T.astype(BF16)


def panel_piece(quantized, exponents, at, piece):
    blocks = exponents.shape[1]
    return pl.pallas_call(
        panel_kernel,
        out_shape=jax.ShapeDtypeStruct((PANEL, piece), BF16),
        grid_spec=pltpu.PrefetchScalarGridSpec(
            num_scalar_prefetch=1,
            grid=(1,),
            in_specs=[
                pl.BlockSpec((piece, PANEL), lambda i, place: (place[0], 0)),
                pl.BlockSpec((piece, blocks), lambda i, place: (place[0], 0)),
            ],
            out_specs=pl.BlockSpec((PANEL, piece), lambda i, place: (0, 0)),
        ),
        compiler_params=pltpu.CompilerParams(vmem_limit_bytes=48 * MIB),
        cost_estimate=pl.CostEstimate(
            flops=piece * PANEL, bytes_accessed=4 * piece * PANEL, transcendentals=0
        ),
    )(at.reshape(1).astype(jnp.int32), quantized, exponents)


def head_kernel(count, *refs):
    total = refs[count][...] if len(refs) > count + 1 else jnp.zeros((PANEL, PANEL), F32)
    for panel_ref in refs[:count]:
        panel = panel_ref[...]
        total += lax.dot_general(
            panel, panel, (((1,), (1,)), ((), ())), preferred_element_type=F32
        )
    refs[-1][...] = total


def head_block(panels, extra=None):
    args = list(panels) + ([] if extra is None else [extra])
    tokens = sum(panel.shape[1] for panel in panels)
    return pl.pallas_call(
        functools.partial(head_kernel, len(panels)),
        out_shape=jax.ShapeDtypeStruct((PANEL, PANEL), F32),
        compiler_params=pltpu.CompilerParams(vmem_limit_bytes=32 * MIB),
        cost_estimate=pl.CostEstimate(
            flops=2 * tokens * PANEL * PANEL, bytes_accessed=2 * tokens * PANEL, transcendentals=0
        ),
    )(*args)


def gram_kernel(width, place_ref, rows_ref, own_ref, other_ref, quant_ref, *refs):
    out_ref, held_ref, sems = refs[-3:]
    steps, _, piece, _ = held_ref.shape
    blocks = width // QBLOCK
    col = place_ref[1]

    def read(k, side):
        at = lax.rem(place_ref[0] + side, 2) * steps + k
        return pltpu.make_async_copy(
            quant_ref.at[
                pl.ds(pl.multiple_of(at * piece, piece), piece),
                pl.ds(pl.multiple_of(col * width, QBLOCK), width),
            ],
            held_ref.at[k, side],
            sems.at[k, side],
        )

    for k in range(steps):
        for side in range(2):
            read(k, side).start()
    out_ref[...] = refs[0][...] if len(refs) > 3 else jnp.zeros_like(out_ref)
    for k in range(steps):
        for side in range(2):
            read(k, side).wait()
            at = lax.rem(place_ref[0] + side, 2) * steps + k
            rows = rows_ref[
                pl.ds(pl.multiple_of(8 * col, 8), 8),
                pl.ds(pl.multiple_of(at * piece, piece), piece),
            ]
            turned = rows.T
            panel = (own_ref, other_ref)[side][:, k * piece : (k + 1) * piece]
            for c in range(0, blocks, 2):
                left = panel * jnp.broadcast_to(rows[c : c + 1].astype(BF16), (PANEL, piece))
                right = held_ref[k, side, :, c * QBLOCK : (c + 1) * QBLOCK]
                if c + 1 < blocks:
                    ratio = jnp.broadcast_to(turned[:, c + 1 : c + 2], (piece, QBLOCK))
                    second = held_ref[k, side, :, (c + 1) * QBLOCK : (c + 2) * QBLOCK]
                    right = jnp.concatenate([right, second * ratio.astype(BF16)], axis=1)
                span = slice(c * QBLOCK, c * QBLOCK + right.shape[1])
                out_ref[:, span] += jnp.dot(left, right, preferred_element_type=F32)


def gram_block(quantized, exponents, scale_rows, own, other, row, col, width, extra=None):
    tokens, _ = quantized.shape
    if scale_rows is None:
        panel = jnp.concatenate([own, other], axis=1)
        quant = lax.dynamic_slice_in_dim(quantized, col * width, width, 1)
        scale = jnp.exp2(exponents.astype(F32)).astype(BF16)
        acts = quant * jnp.take(scale, (col * width + jnp.arange(width)) // QBLOCK, axis=1)
        acts = jnp.roll(acts, -row * (tokens // 2), axis=0)
        total = jnp.dot(panel, acts, preferred_element_type=F32)
        return total if extra is None else total + extra
    piece = tokens // 2 // ROUNDS
    place = jnp.stack([row, col]).astype(jnp.int32)
    vmem = pl.BlockSpec(memory_space=pltpu.VMEM)
    args = [place, scale_rows, own, other, quantized] + ([] if extra is None else [extra])
    specs = [pl.BlockSpec(memory_space=pltpu.SMEM)] + [vmem] * (len(args) - 1)
    specs[4] = pl.BlockSpec(memory_space=pl.ANY)
    return pl.pallas_call(
        functools.partial(gram_kernel, width),
        out_shape=jax.ShapeDtypeStruct((PANEL, width), F32),
        in_specs=specs,
        out_specs=vmem,
        scratch_shapes=[
            pltpu.VMEM((ROUNDS, 2, piece, width), BF16),
            pltpu.SemaphoreType.DMA((ROUNDS, 2)),
        ],
        compiler_params=pltpu.CompilerParams(vmem_limit_bytes=32 * MIB),
        cost_estimate=pl.CostEstimate(
            flops=2 * tokens * width * PANEL,
            bytes_accessed=2 * tokens * width + 4 * PANEL * width,
            transcendentals=0,
        ),
    )(*args)


def inverse_kernel(head_ref, out_ref, pair_ref):
    size = PANEL
    rows = lax.broadcasted_iota(jnp.int32, (size, size), 0)
    cols = lax.broadcasted_iota(jnp.int32, (size, size), 1)
    eye = jnp.where(rows == cols, 1.0, 0.0).astype(F32)
    head = head_ref[...]
    damping = 0.01 * (jnp.sum(head * eye) / size)
    block = head + damping * eye
    high = jnp.max(jnp.sum(jnp.abs(block), axis=0))
    start = 2.0 / (high + damping)
    spread = (high - damping) / (high + damping)
    pair_ref[:size] = start * eye
    pair_ref[size:] = start * block

    def more(spread):
        return spread > 1e-3

    def step(spread):
        square = spread * spread
        gain = 2.0 / (2.0 - square)
        turn = gain * (2.0 * eye - pair_ref[size:])
        pair_ref[...] = dot_high(pair_ref[...], turn)
        return square / (2.0 - square)

    lax.while_loop(more, step, spread)
    out = pair_ref[:size]
    for _ in range(2):
        out = out + dot_high(out, eye - dot_high(block, out))
    out_ref[...] = out


def invert(head):
    return pl.pallas_call(
        inverse_kernel,
        out_shape=jax.ShapeDtypeStruct((PANEL, PANEL), F32),
        scratch_shapes=[pltpu.VMEM((2 * PANEL, PANEL), F32)],
        compiler_params=pltpu.CompilerParams(vmem_limit_bytes=32 * MIB),
        cost_estimate=pl.CostEstimate(
            flops=28 * 12 * PANEL**3, bytes_accessed=8 * PANEL * PANEL, transcendentals=0
        ),
    )(head)


def gains_kernel(inverse_ref, first_ref, second_ref, third_ref, high_ref, pair_ref):
    total = first_ref[...] + second_ref[...] + third_ref[...]
    gains = dot_high(inverse_ref[...], total)
    high = gains.astype(BF16)
    high_ref[...] = high
    pair_ref[:PANEL] = high
    pair_ref[PANEL:] = (gains - high.astype(F32)).astype(BF16)


def make_gains(inverse, parts):
    width = parts[0].shape[1]
    return pl.pallas_call(
        gains_kernel,
        out_shape=(
            jax.ShapeDtypeStruct((PANEL, width), BF16),
            jax.ShapeDtypeStruct((2 * PANEL, width), BF16),
        ),
        compiler_params=pltpu.CompilerParams(vmem_limit_bytes=32 * MIB),
        cost_estimate=pl.CostEstimate(
            flops=12 * PANEL * PANEL * width, bytes_accessed=16 * PANEL * width, transcendentals=0
        ),
    )(inverse, *parts)


def update_kernel(shapes, place_ref, error_ref, weights_ref, *refs):
    count = len(shapes)
    groups, at = [], 0
    for pieces in shapes:
        groups.append(refs[at : at + len(pieces)])
        at += len(pieces)
    out_ref, made_ref, made_sems = refs[-3:]
    _, parts, step, width = made_ref.shape

    def columns(j):
        return pl.ds(pl.multiple_of(place_ref[j] * width, QBLOCK), width)

    def made(j, i):
        return pltpu.make_async_copy(
            made_ref.at[j, i],
            out_ref.at[pl.ds(i * step, step), columns(j)],
            made_sems.at[j, i],
        )

    spots = [(j, i) for j in range(count) for i in range(parts)]
    for j, i in spots:
        error = error_ref[i * step : (i + 1) * step, :]
        total = weights_ref[i * step : (i + 1) * step, columns(j)].astype(F32)
        row = 0
        for gain in groups[j]:
            for top in range(0, gain.shape[0], PANEL):
                size = min(PANEL, gain.shape[0])
                total += jnp.dot(
                    error[:, row : row + size],
                    gain[top : top + size, :],
                    preferred_element_type=F32,
                )
                row = (row + size) % PANEL
        made_ref[j, i] = total.astype(BF16)

        @pl.when(place_ref[count + j] == 1)
        def _():
            made_ref[j, i, :, :PANEL] = weights_ref[i * step : (i + 1) * step, :PANEL] - error

        made(j, i).start()
    for j, i in spots:
        made(j, i).wait()


def update_blocks(out, weights, error, gains, spots, first):
    rows, cols = weights.shape
    width = gains[0][0].shape[1]
    count = len(gains)
    if width % QBLOCK or width < PANEL:
        out = jnp.zeros_like(weights) if out is None else out
        for pieces, col in zip(gains, spots):
            total = lax.dynamic_slice_in_dim(weights, col * width, width, 1).astype(F32)
            gain = jnp.concatenate(pieces, axis=0)
            for at in range(0, gain.shape[0], PANEL):
                total += jnp.dot(error, gain[at : at + PANEL], preferred_element_type=F32)
            out = lax.dynamic_update_slice_in_dim(out, total.astype(BF16), col * width, 1)
        return out
    parts = 4 if rows % 64 == 0 else 1
    place = jnp.stack(list(spots) + [first & (col == 0) for col in spots]).astype(jnp.int32)
    flat = [piece for pieces in gains for piece in pieces]
    vmem, anywhere = pl.BlockSpec(memory_space=pltpu.VMEM), pl.BlockSpec(memory_space=pl.ANY)
    specs = [pl.BlockSpec(memory_space=pltpu.SMEM), vmem, vmem] + [vmem] * len(flat)
    args = [place, error, weights, *flat]
    aliases = {}
    if out is not None:
        specs.append(anywhere)
        aliases = {len(args): 0}
        args.append(out)
    buffer = pltpu.VMEM((count, parts, rows // parts, width), BF16)
    sems = pltpu.SemaphoreType.DMA((count, parts))
    return pl.pallas_call(
        functools.partial(update_kernel, [[p.shape for p in pieces] for pieces in gains]),
        out_shape=jax.ShapeDtypeStruct((rows, cols), BF16),
        in_specs=specs,
        out_specs=anywhere,
        scratch_shapes=[buffer, sems],
        input_output_aliases=aliases,
        compiler_params=pltpu.CompilerParams(vmem_limit_bytes=48 * MIB),
        cost_estimate=pl.CostEstimate(
            flops=2 * rows * width * PANEL * count,
            bytes_accessed=4 * rows * width * count,
            transcendentals=0,
        ),
    )(*args)


def swap(x, axis, bit):
    size = lax.axis_size(axis)
    return lax.ppermute(x, axis, [(i, i ^ bit) for i in range(size)])


def after(x, *others):
    return lax.optimization_barrier((x, *others))[0]


def shards(quantized, exponents, weights, keep_mask):
    tokens, cols = quantized.shape
    toks, rows, feats = lax.axis_size("tok"), lax.axis_size("row"), lax.axis_size("feat")
    tok, row, feat = lax.axis_index("tok"), lax.axis_index("row"), lax.axis_index("feat")
    width = cols // (toks * rows)
    root = feat == 0

    piece = tokens // rows // ROUNDS
    sources = [
        panel_piece(quantized, exponents, row * ROUNDS + c, piece) for c in range(ROUNDS)
    ]
    error = jnp.where(keep_mask == 0, weights[:, :PANEL], jnp.zeros((), BF16)).T
    extras = -(-error.shape[1] // piece)
    error = jnp.pad(error, ((0, 0), (0, extras * piece - error.shape[1])))
    sources += [error[:, i * piece : (i + 1) * piece] for i in range(extras)]
    count, hops = len(sources), feats - 1
    events = [(c - 2.5, 0, c, -1) for c in range(count)]
    events += [(c + h, 1 - h, c, h) for c in range(count) for h in range(hops)]
    got = [[x] for x in sources]
    full = [None] * count
    swapped = [None] * ROUNDS
    token = None

    def settle(c):
        result = sources[c]
        for hop in range(hops):
            result = jnp.where(feat == hop + 1, got[c][hop + 1], result)
        return result

    rest = []
    for when, _, c, h in sorted(events):
        if when > ROUNDS + hops - 2:
            rest.append((c, h))
            continue
        x = got[c][h + 1]
        if token is not None:
            x = after(x, token)
        got[c][h + 1] = token = x
        if h + 1 < hops:
            got[c].append(lax.ppermute(x, "feat", [(h + 1, h + 2)]))
        elif c < ROUNDS:
            full[c] = settle(c)
            swapped[c] = swap(full[c], "row", 1)

    def later(link):
        for c, h in rest:
            x = after(got[c][h + 1], link)
            if h + 1 < hops:
                got[c].append(lax.ppermute(x, "feat", [(h + 1, h + 2)]))

    scale_rows = None
    if width % QBLOCK == 0 and width // QBLOCK <= 8:
        blocks = width // QBLOCK
        exps = after(exponents, got[1][1]).T.reshape(toks * rows, blocks, tokens)
        before = jnp.pad(exps[:, :-1], ((0, 0), (1, 0), (0, 0)))
        odd = (jnp.arange(blocks) % 2 == 1)[None, :, None]
        exps = jnp.where(odd, exps - before, exps)
        exps = jnp.pad(exps, ((0, 0), (0, 8 - blocks), (0, 0)))
        scale_rows = jnp.exp2(exps.astype(F32)).reshape(-1, tokens)

    head = head_block(full[: ROUNDS - 1] + swapped[:-1])
    last = after(swapped[-1], head)
    own = jnp.concatenate(full[:ROUNDS], axis=1)
    other = jnp.concatenate(swapped[:-1] + [last], axis=1)

    def gram(k, extra=None):
        col = row * toks + (tok ^ k)
        return gram_block(
            quantized, exponents, scale_rows, own, other, row, col, width, extra
        )

    head = head_block([full[ROUNDS - 1], last], head)
    head = head + swap(head, "tok", 1)
    block3 = gram(3)
    from3 = swap(block3, "tok", 1)
    later(block3)
    head = head + swap(head, "tok", 2)
    block2, head = lax.optimization_barrier((gram(2, from3), head))
    fromx = swap(block2, "tok", 2)
    from1 = swap(gram(1), "tok", 1)
    block0 = gram(0)
    inverse = invert(head)
    error = jnp.concatenate([settle(c) for c in range(ROUNDS, count)], axis=1)
    error = error[:, : weights.shape[0]].T
    inverse, error = lax.optimization_barrier((inverse, error))
    high, pair = make_gains(inverse, (block0, from1, fromx))

    half = PANEL // 2

    def update(out, group):
        spots = [(row ^ row_bit) * toks + (tok ^ tok_bits) for _, tok_bits, row_bit in group]
        return update_blocks(out, weights, error, [gain for gain, _, _ in group], spots, root)

    near = swap(pair, "tok", 1)
    in_x, in_y = swap(high, "tok", 2), swap(high, "row", 1)
    out = update(None, [((pair,), 0, 0), ((near,), 1, 0)])
    in_x, in_y, out = lax.optimization_barrier((in_x, in_y, out))
    far = (swap(in_y[:half], "tok", 2), swap(in_x[half:], "row", 1))
    near_x, near_y = swap(in_x, "tok", 1), swap(in_y, "tok", 1)
    near_far = tuple(swap(x, "tok", 1) for x in far)
    out = update(
        out, [((in_x,), 2, 0), ((in_y,), 0, 1), ((near_x,), 3, 0), ((near_y,), 1, 1)]
    )
    out = update(out, [(far, 2, 1), (near_far, 3, 1)])
    if width % QBLOCK or width < PANEL:
        panel = jnp.where(root, weights[:, :PANEL] - error, out[:, :PANEL])
        out = lax.dynamic_update_slice_in_dim(out, panel, 0, 1)
    return out


def solution(mesh):
    placed = (
        P("tok", "feat"),
        P("tok", "feat"),
        P(("tok", "row"), "feat"),
        P(("tok", "row"), None),
    )
    return jax.shard_map(
        shards, mesh=mesh, in_specs=placed, out_specs=P(("tok", "row"), "feat"), check_vma=False
    )
```

```python
import functools

import jax
import jax.numpy as jnp
from jax import lax
from jax.experimental import pallas as pl
from jax.experimental.pallas import tpu as pltpu
from jax.sharding import PartitionSpec as P

PANEL = 256
QBLOCK = 128
ROUNDS = 4
F32 = jnp.float32
BF16 = jnp.bfloat16
MIB = 1 << 20


def dot_high(left, right):
    return jnp.dot(left, right, precision=lax.Precision.HIGHEST, preferred_element_type=F32)


def panel_kernel(place_ref, quant_ref, exps_ref, out_ref):
    scale = jnp.exp2(exps_ref[:, : PANEL // QBLOCK].astype(F32))
    rows = scale.shape[0]
    wide = [
        jnp.broadcast_to(scale[:, c : c + 1], (rows, QBLOCK)) for c in range(PANEL // QBLOCK)
    ]
    acts = quant_ref[...].astype(F32) * jnp.concatenate(wide, axis=1)
    out_ref[...] = acts.T.astype(BF16)


def panel_piece(quantized, exponents, at, piece):
    blocks = exponents.shape[1]
    return pl.pallas_call(
        panel_kernel,
        out_shape=jax.ShapeDtypeStruct((PANEL, piece), BF16),
        grid_spec=pltpu.PrefetchScalarGridSpec(
            num_scalar_prefetch=1,
            grid=(1,),
            in_specs=[
                pl.BlockSpec((piece, PANEL), lambda i, place: (place[0], 0)),
                pl.BlockSpec((piece, blocks), lambda i, place: (place[0], 0)),
            ],
            out_specs=pl.BlockSpec((PANEL, piece), lambda i, place: (0, 0)),
        ),
        compiler_params=pltpu.CompilerParams(vmem_limit_bytes=48 * MIB),
        cost_estimate=pl.CostEstimate(
            flops=piece * PANEL, bytes_accessed=4 * piece * PANEL, transcendentals=0
        ),
    )(at.reshape(1).astype(jnp.int32), quantized, exponents)


def inverse_kernel(head_ref, out_ref, pair_ref):
    size = PANEL
    rows = lax.broadcasted_iota(jnp.int32, (size, size), 0)
    cols = lax.broadcasted_iota(jnp.int32, (size, size), 1)
    eye = jnp.where(rows == cols, 1.0, 0.0).astype(F32)
    head = head_ref[...]
    damping = 0.01 * (jnp.sum(head * eye) / size)
    block = head + damping * eye
    high = jnp.max(jnp.sum(jnp.abs(block), axis=0))
    start = 2.0 / (high + damping)
    spread = (high - damping) / (high + damping)
    pair_ref[:size] = start * eye
    pair_ref[size:] = start * block

    def more(spread):
        return spread > 1e-3

    def step(spread):
        square = spread * spread
        gain = 2.0 / (2.0 - square)
        turn = gain * (2.0 * eye - pair_ref[size:])
        pair_ref[...] = dot_high(pair_ref[...], turn)
        return square / (2.0 - square)

    lax.while_loop(more, step, spread)
    out = pair_ref[:size]
    for _ in range(2):
        out = out + dot_high(out, eye - dot_high(block, out))
    out_ref[...] = out


def invert(head):
    return pl.pallas_call(
        inverse_kernel,
        out_shape=jax.ShapeDtypeStruct((PANEL, PANEL), F32),
        scratch_shapes=[pltpu.VMEM((2 * PANEL, PANEL), F32)],
        compiler_params=pltpu.CompilerParams(vmem_limit_bytes=32 * MIB),
        cost_estimate=pl.CostEstimate(
            flops=28 * 12 * PANEL**3, bytes_accessed=8 * PANEL * PANEL, transcendentals=0
        ),
    )(head)


def gains_kernel(place_ref, inverse_ref, first_ref, second_ref, third_ref, high_ref, pair_ref):
    total = first_ref[...] + second_ref[...] + third_ref[...]
    gains = dot_high(inverse_ref[...], total)
    rows = lax.broadcasted_iota(jnp.int32, gains.shape, 0)
    cols = lax.broadcasted_iota(jnp.int32, gains.shape, 1) + place_ref[0]
    gains = jnp.where(cols < PANEL, jnp.where(rows == cols, -1.0, 0.0), gains)
    high = gains.astype(BF16)
    high_ref[...] = high
    pair_ref[:PANEL] = high
    pair_ref[PANEL:] = (gains - high.astype(F32)).astype(BF16)


def make_gains(inverse, parts, start):
    width = parts[0].shape[1]
    vmem = pl.BlockSpec(memory_space=pltpu.VMEM)
    return pl.pallas_call(
        gains_kernel,
        out_shape=(
            jax.ShapeDtypeStruct((PANEL, width), BF16),
            jax.ShapeDtypeStruct((2 * PANEL, width), BF16),
        ),
        in_specs=[pl.BlockSpec(memory_space=pltpu.SMEM)] + [vmem] * 4,
        compiler_params=pltpu.CompilerParams(vmem_limit_bytes=32 * MIB),
        cost_estimate=pl.CostEstimate(
            flops=12 * PANEL * PANEL * width, bytes_accessed=16 * PANEL * width, transcendentals=0
        ),
    )(start.reshape(1).astype(jnp.int32), inverse, *parts)


def swap(x, axis, bit):
    size = lax.axis_size(axis)
    return lax.ppermute(x, axis, [(i, i ^ bit) for i in range(size)])


def forward(x, axis):
    size = lax.axis_size(axis)
    return lax.ppermute(x, axis, [(i, i + 1) for i in range(size - 1)])


def after(x, *others):
    return lax.optimization_barrier((x, *others))[0]


def dot(left, right):
    return jnp.dot(left, right, preferred_element_type=F32)


def shards(quantized, exponents, weights, keep_mask):
    tokens, cols = quantized.shape
    toks, rows, feats = lax.axis_size("tok"), lax.axis_size("row"), lax.axis_size("feat")
    tok, row, feat = lax.axis_index("tok"), lax.axis_index("row"), lax.axis_index("feat")
    width = cols // (toks * rows)
    root = feat == 0

    piece = tokens // rows // ROUNDS
    sources = [
        panel_piece(quantized, exponents, row * ROUNDS + c, piece) for c in range(ROUNDS)
    ]
    panel_weights = after(weights[:, :PANEL], sources[0])
    error = jnp.where(keep_mask == 0, panel_weights, jnp.zeros((), BF16)).T
    extras = -(-error.shape[1] // piece)
    error = jnp.pad(error, ((0, 0), (0, extras * piece - error.shape[1])))
    sources += [error[:, i * piece : (i + 1) * piece] for i in range(extras)]
    panel_rounds = ROUNDS + feats - 1
    held, swapped = [jnp.where(root, sources[0], jnp.zeros((), BF16))], []

    def advance(*others):
        r = len(held)
        x = forward(after(held[-1], *others) if others else held[-1], "feat")
        held.append(jnp.where(root, sources[r], x) if r < len(sources) else x)

    for r in range(1, panel_rounds):
        swapped.append(swap(held[r - 1], "row", 1))
        advance(*swapped[r - 2 : r - 1])
    swapped.append(swap(held[-1], "row", 1))

    scale = jnp.exp2(after(exponents, sources[0]).astype(F32)).astype(BF16)
    acts = []
    for k, link in zip((3, 2, 1, 0), (1, 2, 3, 4)):
        col = row * toks + (tok ^ k)
        block = (col * width + lax.broadcasted_iota(jnp.int32, (1, width), 1)) // QBLOCK
        spread = lax.broadcasted_iota(jnp.int32, (scale.shape[1], width), 0) == block
        wide = dot(after(scale, held[link]), spread.astype(BF16)).astype(BF16)
        acts.insert(0, lax.dynamic_slice_in_dim(quantized, col * width, width, 1) * wide)

    def window(rounds, first, count):
        rounds = jnp.concatenate(rounds, axis=1)
        return lax.dynamic_slice_in_dim(rounds, first * piece, count * piece, 1)

    own = window(held[:panel_rounds], feat, ROUNDS)
    other = window(swapped, feat, ROUNDS)
    panel = jnp.concatenate(
        [jnp.where(row == 0, own, other), jnp.where(row == 0, other, own)], axis=1
    )

    head = lax.dot_general(
        panel, panel, (((1,), (1,)), ((), ())), preferred_element_type=F32
    )
    head = head + swap(head, "tok", 1)
    block3 = dot(panel, acts[3])
    from3 = swap(block3, "tok", 1)
    head = head + swap(head, "tok", 2)
    advance(block3)
    block2 = dot(panel, acts[2]) + from3
    block2, head = lax.optimization_barrier((block2, head))
    fromx = swap(block2, "tok", 2)
    block1 = dot(panel, acts[1])
    from1 = swap(block1, "tok", 1)
    block0 = dot(panel, acts[0])
    while len(held) < len(sources) + feats - 1:
        advance(block1)
    inverse = invert(after(head, held[-1]))
    error = window(held[ROUNDS:], feat, extras)[:, : weights.shape[0]].T
    inverse, error = lax.optimization_barrier((inverse, error))
    start = jnp.where(root, (row * toks + tok) * width, PANEL)
    high, pair = make_gains(inverse, (block0, from1, fromx), start)

    half = PANEL // 2

    def update(out, gain, tok_bits, row_bit):
        start = ((row ^ row_bit) * toks + (tok ^ tok_bits)) * width
        total = lax.dynamic_slice_in_dim(weights, start, width, 1).astype(F32)
        for top in range(0, gain.shape[0], PANEL):
            total = total + dot(error, gain[top : top + PANEL])
        return lax.dynamic_update_slice_in_dim(out, total.astype(BF16), start, 1)

    near = swap(pair, "tok", 1)
    in_x, in_y = swap(high, "tok", 2), swap(high, "row", 1)
    out = jnp.zeros_like(weights)
    out = update(out, pair, 0, 0)
    out = update(out, near, 1, 0)
    in_x, in_y, out = lax.optimization_barrier((in_x, in_y, out))
    far = jnp.concatenate([swap(in_y[:half], "tok", 2), swap(in_x[half:], "row", 1)], axis=0)
    near_x, near_y = swap(in_x, "tok", 1), swap(in_y, "tok", 1)
    out = update(out, in_x, 2, 0)
    out = update(out, in_y, 0, 1)
    far, out = lax.optimization_barrier((far, out))
    near_far = swap(far, "tok", 1)
    out = update(out, near_x, 3, 0)
    out = update(out, near_y, 1, 1)
    out = update(out, far, 2, 1)
    return update(out, near_far, 3, 1)


def solution(mesh):
    placed = (
        P("tok", "feat"),
        P("tok", "feat"),
        P(("tok", "row"), "feat"),
        P(("tok", "row"), None),
    )
    return jax.shard_map(
        shards, mesh=mesh, in_specs=placed, out_specs=P(("tok", "row"), "feat"), check_vma=False
    )
```

```python
import functools

import jax
import jax.numpy as jnp
from jax import lax
from jax.experimental import pallas as pl
from jax.experimental.pallas import tpu as pltpu
from jax.sharding import PartitionSpec as P

PANEL = 256
QBLOCK = 128
ROUNDS = 4
F32 = jnp.float32
BF16 = jnp.bfloat16
MIB = 1 << 20


def dot_high(left, right):
    return jnp.dot(left, right, precision=lax.Precision.HIGHEST, preferred_element_type=F32)


def panel_kernel(place_ref, quant_ref, exps_ref, out_ref):
    scale = jnp.exp2(exps_ref[:, : PANEL // QBLOCK].astype(F32))
    rows = scale.shape[0]
    wide = [
        jnp.broadcast_to(scale[:, c : c + 1], (rows, QBLOCK)) for c in range(PANEL // QBLOCK)
    ]
    acts = quant_ref[...].astype(F32) * jnp.concatenate(wide, axis=1)
    out_ref[...] = acts.T.astype(BF16)


def panel_piece(quantized, exponents, at, piece):
    blocks = exponents.shape[1]
    return pl.pallas_call(
        panel_kernel,
        out_shape=jax.ShapeDtypeStruct((PANEL, piece), BF16),
        grid_spec=pltpu.PrefetchScalarGridSpec(
            num_scalar_prefetch=1,
            grid=(1,),
            in_specs=[
                pl.BlockSpec((piece, PANEL), lambda i, place: (place[0], 0)),
                pl.BlockSpec((piece, blocks), lambda i, place: (place[0], 0)),
            ],
            out_specs=pl.BlockSpec((PANEL, piece), lambda i, place: (0, 0)),
        ),
        compiler_params=pltpu.CompilerParams(vmem_limit_bytes=48 * MIB),
        cost_estimate=pl.CostEstimate(
            flops=piece * PANEL, bytes_accessed=4 * piece * PANEL, transcendentals=0
        ),
    )(at.reshape(1).astype(jnp.int32), quantized, exponents)


def inverse_kernel(head_ref, out_ref, pair_ref):
    size = PANEL
    rows = lax.broadcasted_iota(jnp.int32, (size, size), 0)
    cols = lax.broadcasted_iota(jnp.int32, (size, size), 1)
    eye = jnp.where(rows == cols, 1.0, 0.0).astype(F32)
    head = head_ref[...]
    damping = 0.01 * (jnp.sum(head * eye) / size)
    block = head + damping * eye
    high = jnp.max(jnp.sum(jnp.abs(block), axis=0))
    start = 2.0 / (high + damping)
    spread = (high - damping) / (high + damping)
    pair_ref[:size] = start * eye
    pair_ref[size:] = start * block

    def more(spread):
        return spread > 1e-3

    def step(spread):
        square = spread * spread
        gain = 2.0 / (2.0 - square)
        turn = gain * (2.0 * eye - pair_ref[size:])
        pair_ref[...] = dot_high(pair_ref[...], turn)
        return square / (2.0 - square)

    lax.while_loop(more, step, spread)
    out = pair_ref[:size]
    for _ in range(2):
        out = out + dot_high(out, eye - dot_high(block, out))
    out_ref[...] = out


def invert(head):
    return pl.pallas_call(
        inverse_kernel,
        out_shape=jax.ShapeDtypeStruct((PANEL, PANEL), F32),
        scratch_shapes=[pltpu.VMEM((2 * PANEL, PANEL), F32)],
        compiler_params=pltpu.CompilerParams(vmem_limit_bytes=32 * MIB),
        cost_estimate=pl.CostEstimate(
            flops=28 * 12 * PANEL**3, bytes_accessed=8 * PANEL * PANEL, transcendentals=0
        ),
    )(head)


def gains_kernel(place_ref, inverse_ref, first_ref, second_ref, third_ref, high_ref, pair_ref):
    total = first_ref[...] + second_ref[...] + third_ref[...]
    gains = dot_high(inverse_ref[...], total)
    rows = lax.broadcasted_iota(jnp.int32, gains.shape, 0)
    cols = lax.broadcasted_iota(jnp.int32, gains.shape, 1) + place_ref[0]
    gains = jnp.where(cols < PANEL, jnp.where(rows == cols, -1.0, 0.0), gains)
    high = gains.astype(BF16)
    high_ref[...] = high
    pair_ref[:PANEL] = high
    pair_ref[PANEL:] = (gains - high.astype(F32)).astype(BF16)


def make_gains(inverse, parts, start):
    width = parts[0].shape[1]
    vmem = pl.BlockSpec(memory_space=pltpu.VMEM)
    return pl.pallas_call(
        gains_kernel,
        out_shape=(
            jax.ShapeDtypeStruct((PANEL, width), BF16),
            jax.ShapeDtypeStruct((2 * PANEL, width), BF16),
        ),
        in_specs=[pl.BlockSpec(memory_space=pltpu.SMEM)] + [vmem] * 4,
        compiler_params=pltpu.CompilerParams(vmem_limit_bytes=32 * MIB),
        cost_estimate=pl.CostEstimate(
            flops=12 * PANEL * PANEL * width, bytes_accessed=16 * PANEL * width, transcendentals=0
        ),
    )(start.reshape(1).astype(jnp.int32), inverse, *parts)


def swap(x, axis, bit):
    size = lax.axis_size(axis)
    return lax.ppermute(x, axis, [(i, i ^ bit) for i in range(size)])


def hop(x, axis, start):
    return lax.ppermute(x, axis, [(start, start + 1)])


def after(x, *others):
    return lax.optimization_barrier((x, *others))[0]


def dot(left, right):
    return jnp.dot(left, right, preferred_element_type=F32)


def unwritten(shape, dtype):
    return pl.pallas_call(
        lambda out_ref: None,
        out_shape=jax.ShapeDtypeStruct(shape, dtype),
        out_specs=pl.BlockSpec(memory_space=pl.ANY),
    )()


def shards(quantized, exponents, weights, keep_mask):
    tokens, cols = quantized.shape
    toks, rows, feats = lax.axis_size("tok"), lax.axis_size("row"), lax.axis_size("feat")
    tok, row, feat = lax.axis_index("tok"), lax.axis_index("row"), lax.axis_index("feat")
    width = cols // (toks * rows)
    root = feat == 0
    hops = feats - 1

    piece = tokens // rows // ROUNDS
    got = [
        [panel_piece(quantized, exponents, row * ROUNDS + c, piece)] for c in range(ROUNDS)
    ]
    for c in range(ROUNDS):
        got[c].append(hop(got[c][0], "feat", 0))

    def scaled(k, link):
        scale = jnp.exp2(after(exponents, link).astype(F32)).astype(BF16)
        start = (row * toks + (tok ^ k)) * width
        block = (start + lax.broadcasted_iota(jnp.int32, (1, width), 1)) // QBLOCK
        spread = lax.broadcasted_iota(jnp.int32, (scale.shape[1], width), 0) == block
        wide = dot(scale, spread.astype(BF16)).astype(BF16)
        return lax.dynamic_slice_in_dim(quantized, start, width, 1) * wide

    acts = {3: scaled(3, got[-1][0])}

    def settle(parts):
        result = parts[0]
        for h in range(hops):
            result = jnp.where(feat == h + 1, parts[h + 1], result)
        return result

    events = sorted((5 * (c + 1) + 8 * h, c, h) for c in range(ROUNDS) for h in range(hops))
    full, swapped, token, errors = [], [], acts[3], []
    for _, c, h in events:
        x = after(got[c][h + 1], token)
        got[c][h + 1] = token = x
        if h + 1 < hops:
            got[c].append(hop(x, "feat", h + 1))
        else:
            full.append(settle(got[c]))
            swapped.append(swap(full[-1], "row", 1))
        if (c, h) == (1, 0):
            acts[2] = token = scaled(2, x)
        elif (c, h) == (1, 1):
            acts[1] = token = scaled(1, x)
        elif (c, h) == (0, 1):
            panel_weights, mask = after(weights[:, :PANEL], x), after(keep_mask, x)
            error = jnp.where(mask == 0, panel_weights, jnp.zeros((), BF16)).T
            extras = -(-error.shape[1] // piece)
            error = jnp.pad(error, ((0, 0), (0, extras * piece - error.shape[1])))
            errors = [[error[:, i * piece : (i + 1) * piece]] for i in range(extras)]
        elif (c, h) == (ROUNDS - 1, 0):
            for parts in errors:
                parts[0] = after(parts[0], x)
                parts.append(hop(parts[0], "feat", 0))
        elif (c, h) == (ROUNDS - 1, 1):
            for parts in errors:
                parts[1] = after(parts[1], x)
                parts.append(hop(parts[1], "feat", 1))

    own, other = jnp.concatenate(full, axis=1), jnp.concatenate(swapped, axis=1)
    panel = jnp.concatenate(
        [jnp.where(row == 0, own, other), jnp.where(row == 0, other, own)], axis=1
    )

    head = lax.dot_general(
        panel, panel, (((1,), (1,)), ((), ())), preferred_element_type=F32
    )
    head = head + swap(head, "tok", 1)
    block3 = dot(panel, acts[3])
    from3 = swap(block3, "tok", 1)
    head = head + swap(head, "tok", 2)
    acts[2] = after(acts[2], from3)
    block2 = dot(panel, acts[2]) + from3
    block2, head = lax.optimization_barrier((block2, head))
    fromx = swap(block2, "tok", 2)
    for parts in errors:
        parts[2] = after(parts[2], block2)
        for h in range(2, hops):
            parts.append(hop(parts[h], "feat", h))
    block1 = dot(panel, acts[1])
    from1 = swap(block1, "tok", 1)
    block0 = dot(panel, scaled(0, block1))
    error = jnp.concatenate([settle(parts) for parts in errors], axis=1)
    error = error[:, : weights.shape[0]].T
    twice = jnp.concatenate([error, error], axis=1)
    head, twice = lax.optimization_barrier((head, twice))
    inverse = invert(head)
    start = jnp.where(root, (row * toks + tok) * width, PANEL)
    high, pair = make_gains(inverse, (block0, from1, fromx), start)

    half = PANEL // 2

    def update(out, gain, tok_bits, row_bit):
        start = ((row ^ row_bit) * toks + (tok ^ tok_bits)) * width
        total = lax.dynamic_slice_in_dim(weights, start, width, 1).astype(F32)
        total = total + dot(twice[:, : gain.shape[0]], gain)
        return lax.dynamic_update_slice_in_dim(out, total.astype(BF16), start, 1)

    in_x, in_y = swap(high, "tok", 2), swap(high, "row", 1)
    near = swap(pair, "tok", 1)
    out = unwritten(weights.shape, BF16)
    out = update(out, pair, 0, 0)
    out = update(out, near, 1, 0)
    in_x, in_y, out = lax.optimization_barrier((in_x, in_y, out))
    top, bottom, out = lax.optimization_barrier((in_y[:half], in_x[half:], out))
    far = jnp.concatenate([swap(top, "tok", 2), swap(bottom, "row", 1)], axis=0)
    near_x, near_y = swap(in_x, "tok", 1), swap(in_y, "tok", 1)
    out = update(out, in_x, 2, 0)
    out = update(out, in_y, 0, 1)
    far, out = lax.optimization_barrier((far, out))
    near_far = swap(far, "tok", 1)
    out = update(out, near_x, 3, 0)
    out = update(out, near_y, 1, 1)
    out = update(out, far, 2, 1)
    return update(out, near_far, 3, 1)


def solution(mesh):
    placed = (
        P("tok", "feat"),
        P("tok", "feat"),
        P(("tok", "row"), "feat"),
        P(("tok", "row"), None),
    )
    return jax.shard_map(
        shards, mesh=mesh, in_specs=placed, out_specs=P(("tok", "row"), "feat"), check_vma=False
    )
```

```python
import functools

import jax
import jax.numpy as jnp
from jax import lax
from jax.experimental import pallas as pl
from jax.experimental.pallas import tpu as pltpu
from jax.sharding import PartitionSpec as P

PANEL = 256
QBLOCK = 128
ROUNDS = 4
F32 = jnp.float32
BF16 = jnp.bfloat16
MIB = 1 << 20


def dot_high(left, right):
    return jnp.dot(left, right, precision=lax.Precision.HIGHEST, preferred_element_type=F32)


def panel_kernel(place_ref, quant_ref, exps_ref, out_ref):
    scale = jnp.exp2(exps_ref[:, : PANEL // QBLOCK].astype(F32))
    rows = scale.shape[0]
    wide = [
        jnp.broadcast_to(scale[:, c : c + 1], (rows, QBLOCK)) for c in range(PANEL // QBLOCK)
    ]
    acts = quant_ref[...].astype(F32) * jnp.concatenate(wide, axis=1)
    out_ref[...] = acts.T.astype(BF16)


def panel_piece(quantized, exponents, at, piece):
    blocks = exponents.shape[1]
    return pl.pallas_call(
        panel_kernel,
        out_shape=jax.ShapeDtypeStruct((PANEL, piece), BF16),
        grid_spec=pltpu.PrefetchScalarGridSpec(
            num_scalar_prefetch=1,
            grid=(1,),
            in_specs=[
                pl.BlockSpec((piece, PANEL), lambda i, place: (place[0], 0)),
                pl.BlockSpec((piece, blocks), lambda i, place: (place[0], 0)),
            ],
            out_specs=pl.BlockSpec((PANEL, piece), lambda i, place: (0, 0)),
        ),
        compiler_params=pltpu.CompilerParams(vmem_limit_bytes=8 * MIB),
        cost_estimate=pl.CostEstimate(
            flops=piece * PANEL, bytes_accessed=4 * piece * PANEL, transcendentals=0
        ),
    )(at.reshape(1).astype(jnp.int32), quantized, exponents)


def scale_kernel(place_ref, exps_ref, quant_ref, out_ref, held_ref, sems):
    parts, step, cols = held_ref.shape
    slots, tokens, width = out_ref.shape
    blocks, half = width // QBLOCK, cols // QBLOCK
    tok, row = place_ref[0], place_ref[1]
    base = pl.multiple_of(place_ref[2] * tokens, tokens)

    def read(i):
        return pltpu.make_async_copy(
            quant_ref.at[
                pl.ds(pl.multiple_of(base + i * step, step), step),
                pl.ds(pl.multiple_of(row * cols, QBLOCK), cols),
            ],
            held_ref.at[i],
            sems.at[i],
        )

    for i in range(parts):
        read(i).start()

    @pl.loop(0, parts)
    def _(i):
        read(i).wait()
        exps = exps_ref[pl.ds(pl.multiple_of(base + i * step, step), step), :]
        mine = exps[:, :half]
        for other in range(1, exps.shape[1] // half):
            mine = jnp.where(row == other, exps[:, other * half : (other + 1) * half], mine)
        scale = jnp.exp2(mine.astype(F32))
        rows = pl.ds(pl.multiple_of(i * step, step), step)
        for slot in range(slots):
            for c in range(blocks):
                at = slot * blocks + c
                wide = jnp.broadcast_to(scale[:, at : at + 1], (step, QBLOCK)).astype(BF16)
                out_ref[tok ^ slot, rows, c * QBLOCK : (c + 1) * QBLOCK] = (
                    held_ref[i, :, at * QBLOCK : (at + 1) * QBLOCK] * wide
                )


def scaled_quarter(quantized, exponents, place, link, slots, width, tokens):
    parts = 8
    return pl.pallas_call(
        scale_kernel,
        out_shape=jax.ShapeDtypeStruct((slots, tokens, width), BF16),
        in_specs=[
            pl.BlockSpec(memory_space=pltpu.SMEM),
            pl.BlockSpec(memory_space=pltpu.VMEM),
            pl.BlockSpec(memory_space=pl.ANY),
        ],
        out_specs=pl.BlockSpec(memory_space=pltpu.VMEM),
        scratch_shapes=[
            pltpu.VMEM((parts, tokens // parts, slots * width), BF16),
            pltpu.SemaphoreType.DMA((parts,)),
        ],
        compiler_params=pltpu.CompilerParams(vmem_limit_bytes=12 * MIB),
        cost_estimate=pl.CostEstimate(
            flops=tokens * width, bytes_accessed=tokens * width, transcendentals=0
        ),
    )(after(jnp.stack(place).astype(jnp.int32), link), exponents, quantized)


def gram_kernel(block, quarters, panel_ref, *refs):
    tokens = panel_ref.shape[1] // quarters
    total = None
    for q in range(quarters):
        part = jnp.dot(
            panel_ref[:, q * tokens : (q + 1) * tokens],
            refs[q][block],
            preferred_element_type=F32,
        )
        total = part if total is None else total + part
    refs[-1][...] = total if len(refs) == quarters + 1 else total + refs[quarters][...]


def gram_block(panel, acts, block, extra=None):
    width = acts[0].shape[2]
    args = [panel, *acts] + ([] if extra is None else [extra])
    vmem = pl.BlockSpec(memory_space=pltpu.VMEM)
    return pl.pallas_call(
        functools.partial(gram_kernel, block, len(acts)),
        out_shape=jax.ShapeDtypeStruct((PANEL, width), F32),
        in_specs=[vmem] * len(args),
        out_specs=vmem,
        compiler_params=pltpu.CompilerParams(vmem_limit_bytes=12 * MIB),
        cost_estimate=pl.CostEstimate(
            flops=PANEL * PANEL * width, bytes_accessed=4 * PANEL * width, transcendentals=0
        ),
    )(*args)


def inverse_kernel(head_ref, out_ref, pair_ref):
    size = PANEL
    rows = lax.broadcasted_iota(jnp.int32, (size, size), 0)
    cols = lax.broadcasted_iota(jnp.int32, (size, size), 1)
    eye = jnp.where(rows == cols, 1.0, 0.0).astype(F32)
    head = head_ref[...]
    damping = 0.01 * (jnp.sum(head * eye) / size)
    block = head + damping * eye
    high = jnp.max(jnp.sum(jnp.abs(block), axis=0))
    start = 2.0 / (high + damping)
    spread = (high - damping) / (high + damping)
    pair_ref[:size] = start * eye
    pair_ref[size:] = start * block

    def more(spread):
        return spread > 1e-3

    def step(spread):
        square = spread * spread
        gain = 2.0 / (2.0 - square)
        turn = gain * (2.0 * eye - pair_ref[size:])
        pair_ref[...] = dot_high(pair_ref[...], turn)
        return square / (2.0 - square)

    lax.while_loop(more, step, spread)
    out = pair_ref[:size]
    for _ in range(2):
        out = out + dot_high(out, eye - dot_high(block, out))
    out_ref[...] = out


def invert(head):
    return pl.pallas_call(
        inverse_kernel,
        out_shape=jax.ShapeDtypeStruct((PANEL, PANEL), F32),
        scratch_shapes=[pltpu.VMEM((2 * PANEL, PANEL), F32)],
        compiler_params=pltpu.CompilerParams(vmem_limit_bytes=8 * MIB),
        cost_estimate=pl.CostEstimate(
            flops=2 * PANEL**3, bytes_accessed=8 * PANEL * PANEL, transcendentals=0
        ),
    )(head)


def gains_kernel(place_ref, inverse_ref, first_ref, second_ref, third_ref, high_ref, pair_ref):
    total = first_ref[...] + second_ref[...] + third_ref[...]
    gains = dot_high(inverse_ref[...], total)
    rows = lax.broadcasted_iota(jnp.int32, gains.shape, 0)
    cols = lax.broadcasted_iota(jnp.int32, gains.shape, 1) + place_ref[0]
    gains = jnp.where(cols < PANEL, jnp.where(rows == cols, -1.0, 0.0), gains)
    high = gains.astype(BF16)
    high_ref[...] = high
    pair_ref[:PANEL] = high
    pair_ref[PANEL:] = (gains - high.astype(F32)).astype(BF16)


def make_gains(inverse, parts, start):
    width = parts[0].shape[1]
    vmem = pl.BlockSpec(memory_space=pltpu.VMEM)
    return pl.pallas_call(
        gains_kernel,
        out_shape=(
            jax.ShapeDtypeStruct((PANEL, width), BF16),
            jax.ShapeDtypeStruct((2 * PANEL, width), BF16),
        ),
        in_specs=[pl.BlockSpec(memory_space=pltpu.SMEM)] + [vmem] * 4,
        compiler_params=pltpu.CompilerParams(vmem_limit_bytes=8 * MIB),
        cost_estimate=pl.CostEstimate(
            flops=12 * PANEL * PANEL * width, bytes_accessed=16 * PANEL * width, transcendentals=0
        ),
    )(start.reshape(1).astype(jnp.int32), inverse, *parts)


def swap(x, axis, bit):
    size = lax.axis_size(axis)
    return lax.ppermute(x, axis, [(i, i ^ bit) for i in range(size)])


def hop(x, axis, start):
    return lax.ppermute(x, axis, [(start, start + 1)])


def after(x, *others):
    return lax.optimization_barrier((x, *others))[0]


def dot(left, right):
    return jnp.dot(left, right, preferred_element_type=F32)


def unwritten(shape, dtype):
    return pl.pallas_call(
        lambda out_ref: None,
        out_shape=jax.ShapeDtypeStruct(shape, dtype),
        out_specs=pl.BlockSpec(memory_space=pl.ANY),
    )()


def shards(quantized, exponents, weights, keep_mask):
    tokens, cols = quantized.shape
    toks, rows, feats = lax.axis_size("tok"), lax.axis_size("row"), lax.axis_size("feat")
    tok, row, feat = lax.axis_index("tok"), lax.axis_index("row"), lax.axis_index("feat")
    width = cols // (toks * rows)
    root = feat == 0
    hops = feats - 1

    piece = tokens // rows // ROUNDS
    got = [
        [panel_piece(quantized, exponents, row * ROUNDS + c, piece)] for c in range(ROUNDS)
    ]
    for c in range(ROUNDS):
        got[c].append(hop(got[c][0], "feat", 0))

    quarters = 4
    kernels = width % QBLOCK == 0

    def scaled(q, link):
        if kernels:
            place = (tok, row, jnp.int32(q))
            return scaled_quarter(
                quantized, exponents, place, link, toks, width, tokens // quarters
            )
        span = slice(q * tokens // quarters, (q + 1) * tokens // quarters)
        scale = jnp.exp2(after(exponents, link)[span].astype(F32)).astype(BF16)
        acts = quantized[span] * jnp.repeat(scale, QBLOCK, axis=1)
        starts = [(row * toks + (tok ^ k)) * width for k in range(toks)]
        return jnp.stack([lax.dynamic_slice_in_dim(acts, at, width, 1) for at in starts])

    def gram(k, *extra):
        if kernels:
            return gram_block(panel, acts, k, *extra)
        block = jnp.concatenate([part[k] for part in acts], axis=0)
        return sum(extra, dot(panel, block))

    acts = [scaled(0, got[-1][0])]

    def settle(parts):
        result = parts[0]
        for h in range(hops):
            result = jnp.where(feat == h + 1, parts[h + 1], result)
        return result

    events = sorted((5 * (c + 1) + 8 * h, c, h) for c in range(ROUNDS) for h in range(hops))
    full, swapped, token = [], [], acts[0]
    for _, c, h in events:
        x = after(got[c][h + 1], token)
        got[c][h + 1] = token = x
        if h + 1 < hops:
            got[c].append(hop(x, "feat", h + 1))
        else:
            full.append(settle(got[c]))
            swapped.append(swap(full[-1], "row", 1))
        if (c, h) in ((1, 0), (2, 0), (2, 1)):
            acts.append(scaled(len(acts), x))
            token = acts[-1]
    panel_weights, mask = after(weights[:, :PANEL], full[0]), after(keep_mask, full[0])
    error = jnp.where(mask == 0, panel_weights, jnp.zeros((), BF16)).T
    extras = -(-error.shape[1] // piece)
    error = jnp.pad(error, ((0, 0), (0, extras * piece - error.shape[1])))
    errors = [
        [after(error[:, i * piece : (i + 1) * piece], full[-1], swapped[0])]
        for i in range(extras)
    ]
    for parts in errors:
        parts.append(hop(parts[0], "feat", 0))

    own, other = jnp.concatenate(full, axis=1), jnp.concatenate(swapped, axis=1)
    panel = jnp.concatenate(
        [jnp.where(row == 0, own, other), jnp.where(row == 0, other, own)], axis=1
    )

    head = lax.dot_general(
        panel, panel, (((1,), (1,)), ((), ())), preferred_element_type=F32
    )
    head = head + swap(head, "tok", 1)
    block3 = gram(3)
    from3 = swap(block3, "tok", 1)
    for parts in errors:
        parts[1] = after(parts[1], block3)
        parts.append(hop(parts[1], "feat", 1))
    head = head + swap(head, "tok", 2)
    block2 = gram(2, from3)
    block2, head = lax.optimization_barrier((block2, head))
    fromx = swap(block2, "tok", 2)
    panel = after(panel, block2)
    block1 = gram(1)
    from1 = swap(block1, "tok", 1)
    for parts in errors:
        parts[2] = after(parts[2], block1)
        for h in range(2, hops):
            parts.append(hop(parts[h], "feat", h))
    panel = after(panel, block1)
    block0 = gram(0)
    inverse = invert(after(head, block0))
    error = jnp.concatenate([settle(parts) for parts in errors], axis=1)
    error = after(error[:, : weights.shape[0]].T, inverse)
    twice = jnp.concatenate([error, error], axis=1)
    inverse, twice = lax.optimization_barrier((inverse, twice))
    start = jnp.where(root, (row * toks + tok) * width, PANEL)
    high, pair = make_gains(inverse, (block0, from1, fromx), start)

    half = PANEL // 2

    def update(out, gain, tok_bits, row_bit):
        start = ((row ^ row_bit) * toks + (tok ^ tok_bits)) * width
        total = lax.dynamic_slice_in_dim(weights, start, width, 1).astype(F32)
        total = total + dot(twice[:, : gain.shape[0]], gain)
        return lax.dynamic_update_slice_in_dim(out, total.astype(BF16), start, 1)

    in_x, in_y = swap(high, "tok", 2), swap(high, "row", 1)
    near = swap(pair, "tok", 1)
    out = unwritten(weights.shape, BF16)
    out = update(out, pair, 0, 0)
    out = update(out, near, 1, 0)
    in_x, in_y, out = lax.optimization_barrier((in_x, in_y, out))
    top, bottom, out = lax.optimization_barrier((in_y[:half], in_x[half:], out))
    far = [swap(top, "tok", 2), swap(bottom, "row", 1)]
    near_x, near_y = swap(in_x, "tok", 1), swap(in_y, "tok", 1)
    out = update(after(out, near_x, near_y), in_x, 2, 0)
    out = update(out, in_y, 0, 1)
    far[0], far[1], out = lax.optimization_barrier((far[0], far[1], out))
    far = jnp.concatenate(far, axis=0)
    near_far = swap(far, "tok", 1)
    out = update(out, near_x, 3, 0)
    out = update(out, near_y, 1, 1)
    out = update(out, far, 2, 1)
    return update(out, near_far, 3, 1)


def solution(mesh):
    placed = (
        P("tok", "feat"),
        P("tok", "feat"),
        P(("tok", "row"), "feat"),
        P(("tok", "row"), None),
    )
    return jax.shard_map(
        shards, mesh=mesh, in_specs=placed, out_specs=P(("tok", "row"), "feat"), check_vma=False
    )
```

```python
import functools

import jax
import jax.numpy as jnp
from jax import lax
from jax.experimental import pallas as pl
from jax.experimental.pallas import tpu as pltpu
from jax.sharding import PartitionSpec as P

PANEL = 256
QBLOCK = 128
ROUNDS = 4
F32 = jnp.float32
BF16 = jnp.bfloat16
MIB = 1 << 20


def dot_high(left, right):
    return jnp.dot(left, right, precision=lax.Precision.HIGHEST, preferred_element_type=F32)


def panel_kernel(place_ref, quant_ref, exps_ref, out_ref):
    scale = jnp.exp2(exps_ref[:, : PANEL // QBLOCK].astype(F32))
    rows = scale.shape[0]
    wide = [
        jnp.broadcast_to(scale[:, c : c + 1], (rows, QBLOCK)) for c in range(PANEL // QBLOCK)
    ]
    acts = quant_ref[...].astype(F32) * jnp.concatenate(wide, axis=1)
    out_ref[...] = acts.T.astype(BF16)


def panel_piece(quantized, exponents, at, piece):
    blocks = exponents.shape[1]
    return pl.pallas_call(
        panel_kernel,
        out_shape=jax.ShapeDtypeStruct((PANEL, piece), BF16),
        grid_spec=pltpu.PrefetchScalarGridSpec(
            num_scalar_prefetch=1,
            grid=(1,),
            in_specs=[
                pl.BlockSpec((piece, PANEL), lambda i, place: (place[0], 0)),
                pl.BlockSpec((piece, blocks), lambda i, place: (place[0], 0)),
            ],
            out_specs=pl.BlockSpec((PANEL, piece), lambda i, place: (0, 0)),
        ),
        compiler_params=pltpu.CompilerParams(vmem_limit_bytes=8 * MIB),
        cost_estimate=pl.CostEstimate(
            flops=piece * PANEL, bytes_accessed=4 * piece * PANEL, transcendentals=0
        ),
    )(at.reshape(1).astype(jnp.int32), quantized, exponents)


def gram_kernel(blocks, place_ref, *refs):
    acts_ref, out_ref = refs[-1], refs[-2]
    step, width = refs[0].shape
    shift = lax.rem(QBLOCK - lax.rem(place_ref[1] * blocks, QBLOCK), QBLOCK)

    @pl.when(pl.program_id(0) == 0)
    def _():
        out_ref[...] = refs[6][...] if len(refs) > 8 else jnp.zeros_like(out_ref)

    for side in range(2):
        quant_ref, exps_ref, _ = refs[3 * side : 3 * side + 3]
        scale = jnp.exp2(exps_ref[...].astype(F32))
        rest = jnp.zeros((step, QBLOCK - scale.shape[1]), F32)
        scale = pltpu.roll(jnp.concatenate([scale, rest], axis=1), shift, 1)
        rows = slice(side * step, (side + 1) * step)
        for c in range(blocks):
            span = slice(c * QBLOCK, (c + 1) * QBLOCK)
            wide = jnp.broadcast_to(scale[:, c : c + 1], (step, QBLOCK)).astype(BF16)
            acts_ref[rows, span] = quant_ref[:, span] * wide
    panel = jnp.concatenate([refs[2][...], refs[5][...]], axis=1)
    out_ref[...] += jnp.dot(panel, acts_ref[...], preferred_element_type=F32)


def gram_block(quantized, exponents, own, other, row, col, width, extra=None):
    tokens, cols = quantized.shape
    if width % QBLOCK or cols // QBLOCK >= QBLOCK:
        panel = jnp.concatenate([own, other], axis=1)
        quant = lax.dynamic_slice_in_dim(quantized, col * width, width, 1)
        scale = jnp.exp2(exponents.astype(F32)).astype(BF16)
        acts = quant * jnp.take(scale, (col * width + jnp.arange(width)) // QBLOCK, axis=1)
        acts = jnp.roll(acts, -row * (tokens // 2), axis=0)
        total = jnp.dot(panel, acts, preferred_element_type=F32)
        return total if extra is None else total + extra
    step = tokens // 2 // ROUNDS
    place = jnp.stack([row, col]).astype(jnp.int32)
    specs, args = [], [place]
    for side, panel in enumerate((own, other)):

        def at(k, place, side=side):
            return lax.rem(place[0] + side, 2) * ROUNDS + k

        specs += [
            pl.BlockSpec((step, width), lambda k, place, at=at: (at(k, place), place[1])),
            pl.BlockSpec((step, cols // QBLOCK), lambda k, place, at=at: (at(k, place), 0)),
            pl.BlockSpec((PANEL, step), lambda k, place: (0, k)),
        ]
        args += [quantized, exponents, panel]
    if extra is not None:
        specs.append(pl.BlockSpec((PANEL, width), lambda k, place: (0, 0)))
        args.append(extra)
    return pl.pallas_call(
        functools.partial(gram_kernel, width // QBLOCK),
        out_shape=jax.ShapeDtypeStruct((PANEL, width), F32),
        grid_spec=pltpu.PrefetchScalarGridSpec(
            num_scalar_prefetch=1,
            grid=(ROUNDS,),
            in_specs=specs,
            out_specs=pl.BlockSpec((PANEL, width), lambda k, place: (0, 0)),
            scratch_shapes=[pltpu.VMEM((2 * step, width), BF16)],
        ),
        compiler_params=pltpu.CompilerParams(vmem_limit_bytes=24 * MIB),
        cost_estimate=pl.CostEstimate(
            flops=PANEL * PANEL * width, bytes_accessed=4 * PANEL * width, transcendentals=0
        ),
    )(*args)


def inverse_kernel(head_ref, out_ref, pair_ref):
    size = PANEL
    rows = lax.broadcasted_iota(jnp.int32, (size, size), 0)
    cols = lax.broadcasted_iota(jnp.int32, (size, size), 1)
    eye = jnp.where(rows == cols, 1.0, 0.0).astype(F32)
    head = head_ref[...]
    damping = 0.01 * (jnp.sum(head * eye) / size)
    block = head + damping * eye
    high = jnp.max(jnp.sum(jnp.abs(block), axis=0))
    start = 2.0 / (high + damping)
    spread = (high - damping) / (high + damping)
    pair_ref[:size] = start * eye
    pair_ref[size:] = start * block

    def more(spread):
        return spread > 1e-3

    def step(spread):
        square = spread * spread
        gain = 2.0 / (2.0 - square)
        turn = gain * (2.0 * eye - pair_ref[size:])
        pair_ref[...] = dot_high(pair_ref[...], turn)
        return square / (2.0 - square)

    lax.while_loop(more, step, spread)
    out = pair_ref[:size]
    for _ in range(2):
        out = out + dot_high(out, eye - dot_high(block, out))
    out_ref[...] = out


def invert(head):
    return pl.pallas_call(
        inverse_kernel,
        out_shape=jax.ShapeDtypeStruct((PANEL, PANEL), F32),
        scratch_shapes=[pltpu.VMEM((2 * PANEL, PANEL), F32)],
        compiler_params=pltpu.CompilerParams(vmem_limit_bytes=8 * MIB),
        cost_estimate=pl.CostEstimate(
            flops=2 * PANEL**3, bytes_accessed=8 * PANEL * PANEL, transcendentals=0
        ),
    )(head)


def gains_kernel(place_ref, inverse_ref, first_ref, second_ref, third_ref, high_ref, pair_ref):
    total = first_ref[...] + second_ref[...] + third_ref[...]
    gains = dot_high(inverse_ref[...], total)
    rows = lax.broadcasted_iota(jnp.int32, gains.shape, 0)
    cols = lax.broadcasted_iota(jnp.int32, gains.shape, 1) + place_ref[0]
    gains = jnp.where(cols < PANEL, jnp.where(rows == cols, -1.0, 0.0), gains)
    high = gains.astype(BF16)
    high_ref[...] = high
    pair_ref[:PANEL] = high
    pair_ref[PANEL:] = (gains - high.astype(F32)).astype(BF16)


def make_gains(inverse, parts, start):
    width = parts[0].shape[1]
    vmem = pl.BlockSpec(memory_space=pltpu.VMEM)
    return pl.pallas_call(
        gains_kernel,
        out_shape=(
            jax.ShapeDtypeStruct((PANEL, width), BF16),
            jax.ShapeDtypeStruct((2 * PANEL, width), BF16),
        ),
        in_specs=[pl.BlockSpec(memory_space=pltpu.SMEM)] + [vmem] * 4,
        compiler_params=pltpu.CompilerParams(vmem_limit_bytes=8 * MIB),
        cost_estimate=pl.CostEstimate(
            flops=12 * PANEL * PANEL * width, bytes_accessed=16 * PANEL * width, transcendentals=0
        ),
    )(start.reshape(1).astype(jnp.int32), inverse, *parts)


def update_kernel(shapes, place_ref, error_ref, weights_ref, *refs):
    count = len(shapes)
    groups, at = [], 0
    for pieces in shapes:
        groups.append(refs[at : at + len(pieces)])
        at += len(pieces)
    out_ref, read_ref, made_ref, read_sems, made_sems = refs[-5:]
    _, parts, step, width = read_ref.shape

    def window(ref, j, i):
        col = pl.multiple_of(place_ref[j] * width, QBLOCK)
        return ref.at[pl.ds(i * step, step), pl.ds(col, width)]

    def read(j, i):
        return pltpu.make_async_copy(window(weights_ref, j, i), read_ref.at[j, i], read_sems.at[j, i])

    def made(j, i):
        return pltpu.make_async_copy(made_ref.at[j, i], window(out_ref, j, i), made_sems.at[j, i])

    spots = [(j, i) for j in range(count) for i in range(parts)]
    for j, i in spots:
        read(j, i).start()
    for j, i in spots:
        read(j, i).wait()
        error = error_ref[i * step : (i + 1) * step, :]
        total = read_ref[j, i].astype(F32)
        row = 0
        for gain in groups[j]:
            for top in range(0, gain.shape[0], PANEL):
                size = min(PANEL, gain.shape[0])
                total += jnp.dot(
                    error[:, row : row + size],
                    gain[top : top + size, :],
                    preferred_element_type=F32,
                )
                row = (row + size) % PANEL
        made_ref[j, i] = total.astype(BF16)
        made(j, i).start()
    for j, i in spots:
        made(j, i).wait()


def update_blocks(out, weights, error, gains, spots):
    rows, cols = weights.shape
    width = gains[0][0].shape[1]
    count = len(gains)
    if width % QBLOCK or width < PANEL:
        out = jnp.zeros_like(weights) if out is None else out
        for pieces, col in zip(gains, spots):
            total = lax.dynamic_slice_in_dim(weights, col * width, width, 1).astype(F32)
            gain = jnp.concatenate(pieces, axis=0)
            for at in range(0, gain.shape[0], PANEL):
                total += jnp.dot(error, gain[at : at + PANEL], preferred_element_type=F32)
            out = lax.dynamic_update_slice_in_dim(out, total.astype(BF16), col * width, 1)
        return out
    parts = 4 if rows % 64 == 0 else 1
    place = jnp.stack(spots).astype(jnp.int32)
    flat = [piece for pieces in gains for piece in pieces]
    vmem, anywhere = pl.BlockSpec(memory_space=pltpu.VMEM), pl.BlockSpec(memory_space=pl.ANY)
    specs = [pl.BlockSpec(memory_space=pltpu.SMEM), vmem, anywhere] + [vmem] * len(flat)
    args = [place, error, weights, *flat]
    aliases = {}
    if out is not None:
        specs.append(anywhere)
        aliases = {len(args): 0}
        args.append(out)
    buffer = pltpu.VMEM((count, parts, rows // parts, width), BF16)
    sems = pltpu.SemaphoreType.DMA((count, parts))
    return pl.pallas_call(
        functools.partial(update_kernel, [[p.shape for p in pieces] for pieces in gains]),
        out_shape=jax.ShapeDtypeStruct((rows, cols), BF16),
        in_specs=specs,
        out_specs=anywhere,
        scratch_shapes=[buffer, buffer, sems, sems],
        input_output_aliases=aliases,
        compiler_params=pltpu.CompilerParams(vmem_limit_bytes=36 * MIB),
        cost_estimate=pl.CostEstimate(
            flops=2 * rows * width * PANEL * count,
            bytes_accessed=4 * rows * width * count,
            transcendentals=0,
        ),
    )(*args)


def swap(x, axis, bit):
    size = lax.axis_size(axis)
    return lax.ppermute(x, axis, [(i, i ^ bit) for i in range(size)])


def hop(x, axis, start):
    return lax.ppermute(x, axis, [(start, start + 1)])


def after(x, *others):
    return lax.optimization_barrier((x, *others))[0]


def dot(left, right):
    return jnp.dot(left, right, preferred_element_type=F32)


def shards(quantized, exponents, weights, keep_mask):
    tokens, cols = quantized.shape
    toks, rows, feats = lax.axis_size("tok"), lax.axis_size("row"), lax.axis_size("feat")
    tok, row, feat = lax.axis_index("tok"), lax.axis_index("row"), lax.axis_index("feat")
    width = cols // (toks * rows)
    root = feat == 0
    hops = feats - 1

    piece = tokens // rows // ROUNDS
    got = [
        [panel_piece(quantized, exponents, row * ROUNDS + c, piece)] for c in range(ROUNDS)
    ]
    for c in range(ROUNDS):
        got[c].append(hop(got[c][0], "feat", 0))

    def settle(parts):
        result = parts[0]
        for h in range(hops):
            result = jnp.where(feat == h + 1, parts[h + 1], result)
        return result

    events = sorted((5 * (c + 1) + 8 * h, c, h) for c in range(ROUNDS) for h in range(hops))
    full, swapped, token, errors = [], [], None, None
    for _, c, h in events:
        x = got[c][h + 1]
        if token is not None:
            x = after(x, token)
        if h + 1 == hops and c > 1:
            x = after(x, swapped[c - 2])
        got[c][h + 1] = token = x
        if h + 1 < hops:
            got[c].append(hop(x, "feat", h + 1))
        else:
            full.append(settle(got[c]))
            swapped.append(swap(full[-1], "row", 1))
        if (c, h) == (0, 1):
            panel_weights, mask = after(weights[:, :PANEL], x), after(keep_mask, x)
            error = jnp.where(mask == 0, panel_weights, jnp.zeros((), BF16))
        elif (c, h) == (ROUNDS - 1, 1):
            errors = [after(error, x)]
            errors.append(hop(errors[0], "feat", 0))
    own, other = jnp.concatenate(full, axis=1), jnp.concatenate(swapped, axis=1)

    def gram(k, link, extra=None):
        col = row * toks + (tok ^ k)
        if link is not None:
            col = after(col, link)
        return gram_block(quantized, exponents, own, other, row, col, width, extra)

    head = sum(
        lax.dot_general(x, x, (((1,), (1,)), ((), ())), preferred_element_type=F32)
        for x in (own, other)
    )
    head = head + swap(head, "tok", 1)
    block3 = gram(3, None)
    from3 = swap(block3, "tok", 1)
    errors[1] = after(errors[1], block3)
    errors.append(hop(errors[1], "feat", 1))
    head = head + swap(head, "tok", 2)
    block2 = gram(2, None, from3)
    block2, head = lax.optimization_barrier((block2, head))
    fromx = swap(block2, "tok", 2)
    block1 = gram(1, block2)
    from1 = swap(block1, "tok", 1)
    errors[2] = after(errors[2], block1)
    for h in range(2, hops):
        errors.append(hop(errors[h], "feat", h))
    block0 = gram(0, block1)
    inverse = invert(after(head, block0))
    inverse, last = lax.optimization_barrier((inverse, errors[-1]))
    error = settle(errors[:-1] + [last])
    start = jnp.where(root, (row * toks + tok) * width, PANEL)
    high, pair = make_gains(inverse, (block0, from1, fromx), start)

    half = PANEL // 2

    def update(out, group):
        spots = [(row ^ row_bit) * toks + (tok ^ tok_bits) for _, tok_bits, row_bit in group]
        return update_blocks(out, weights, error, [gain for gain, _, _ in group], spots)

    in_x, in_y = swap(high, "tok", 2), swap(high, "row", 1)
    near = swap(pair, "tok", 1)
    out = update(None, [((pair,), 0, 0), ((near,), 1, 0)])
    in_x, in_y, out = lax.optimization_barrier((in_x, in_y, out))
    top, bottom, out = lax.optimization_barrier((in_y[:half], in_x[half:], out))
    far = [swap(top, "tok", 2), swap(bottom, "row", 1)]
    near_x, near_y = swap(in_x, "tok", 1), swap(in_y, "tok", 1)
    out = update(after(out, near_x, near_y), [((in_x,), 2, 0), ((in_y,), 0, 1)])
    far[0], far[1], out = lax.optimization_barrier((far[0], far[1], out))
    near_far = tuple(swap(x, "tok", 1) for x in far)
    last = [((near_x,), 3, 0), ((near_y,), 1, 1), (tuple(far), 2, 1), (near_far, 3, 1)]
    return update(out, last)


def solution(mesh):
    placed = (
        P("tok", "feat"),
        P("tok", "feat"),
        P(("tok", "row"), "feat"),
        P(("tok", "row"), None),
    )
    return jax.shard_map(
        shards, mesh=mesh, in_specs=placed, out_specs=P(("tok", "row"), "feat"), check_vma=False
    )
```

```python
import functools

import jax
import jax.numpy as jnp
from jax import lax
from jax.experimental import pallas as pl
from jax.experimental.pallas import tpu as pltpu
from jax.sharding import PartitionSpec as P

PANEL = 256
QBLOCK = 128
ROUNDS = 4
F32 = jnp.float32
BF16 = jnp.bfloat16
MIB = 1 << 20


def dot_high(left, right):
    return jnp.dot(left, right, precision=lax.Precision.HIGHEST, preferred_element_type=F32)


def panel_kernel(place_ref, quant_ref, exps_ref, out_ref):
    scale = jnp.exp2(exps_ref[:, : PANEL // QBLOCK].astype(F32))
    rows = scale.shape[0]
    wide = [
        jnp.broadcast_to(scale[:, c : c + 1], (rows, QBLOCK)) for c in range(PANEL // QBLOCK)
    ]
    acts = quant_ref[...].astype(F32) * jnp.concatenate(wide, axis=1)
    out_ref[...] = acts.T.astype(BF16)


def panel_piece(quantized, exponents, at, piece):
    blocks = exponents.shape[1]
    return pl.pallas_call(
        panel_kernel,
        out_shape=jax.ShapeDtypeStruct((PANEL, piece), BF16),
        grid_spec=pltpu.PrefetchScalarGridSpec(
            num_scalar_prefetch=1,
            grid=(1,),
            in_specs=[
                pl.BlockSpec((piece, PANEL), lambda i, place: (place[0], 0)),
                pl.BlockSpec((piece, blocks), lambda i, place: (place[0], 0)),
            ],
            out_specs=pl.BlockSpec((PANEL, piece), lambda i, place: (0, 0)),
        ),
        compiler_params=pltpu.CompilerParams(vmem_limit_bytes=8 * MIB),
        cost_estimate=pl.CostEstimate(
            flops=piece * PANEL, bytes_accessed=4 * piece * PANEL, transcendentals=0
        ),
    )(at.reshape(1).astype(jnp.int32), quantized, exponents)


def gram_kernel(blocks, place_ref, *refs):
    acts_ref, out_ref = refs[-1], refs[-2]
    step, width = refs[0].shape
    shift = lax.rem(QBLOCK - lax.rem(place_ref[1] * blocks, QBLOCK), QBLOCK)

    @pl.when(pl.program_id(0) == 0)
    def _():
        out_ref[...] = refs[6][...] if len(refs) > 8 else jnp.zeros_like(out_ref)

    for side in range(2):
        quant_ref, scale_ref, _ = refs[3 * side : 3 * side + 3]
        scale = pltpu.roll(scale_ref[...], shift, 1)
        rows = slice(side * step, (side + 1) * step)
        for c in range(blocks):
            span = slice(c * QBLOCK, (c + 1) * QBLOCK)
            wide = jnp.broadcast_to(scale[:, c : c + 1], (step, QBLOCK)).astype(BF16)
            acts_ref[rows, span] = quant_ref[:, span] * wide
    panel = jnp.concatenate([refs[2][...], refs[5][...]], axis=1)
    out_ref[...] += jnp.dot(panel, acts_ref[...], preferred_element_type=F32)


def gram_block(quantized, scale_pad, own, other, row, col, width, first, extra=None):
    tokens, cols = quantized.shape
    if width % QBLOCK or cols // QBLOCK > QBLOCK:
        total = 0.0 if extra is None else extra
        for side, panel in enumerate((own, other)):
            at = (row + side) % 2 * (tokens // 2) + first * (tokens // 2 // ROUNDS)
            size = (panel.shape[1], width)
            quant = lax.dynamic_slice(quantized, (at, col * width), size)
            scale = lax.dynamic_slice_in_dim(scale_pad, at, size[0], 0).astype(BF16)
            acts = quant * jnp.take(scale, (col * width + jnp.arange(width)) // QBLOCK, axis=1)
            total = total + jnp.dot(panel, acts, preferred_element_type=F32)
        return total
    step = tokens // 2 // ROUNDS
    place = jnp.stack([row, col]).astype(jnp.int32)
    specs, args = [], [place]
    for side, panel in enumerate((own, other)):

        def at(k, place, side=side):
            return lax.rem(place[0] + side, 2) * ROUNDS + first + k

        specs += [
            pl.BlockSpec((step, width), lambda k, place, at=at: (at(k, place), place[1])),
            pl.BlockSpec((step, QBLOCK), lambda k, place, at=at: (at(k, place), 0)),
            pl.BlockSpec((PANEL, step), lambda k, place: (0, k)),
        ]
        args += [quantized, scale_pad, panel]
    if extra is not None:
        specs.append(pl.BlockSpec((PANEL, width), lambda k, place: (0, 0)))
        args.append(extra)
    return pl.pallas_call(
        functools.partial(gram_kernel, width // QBLOCK),
        out_shape=jax.ShapeDtypeStruct((PANEL, width), F32),
        grid_spec=pltpu.PrefetchScalarGridSpec(
            num_scalar_prefetch=1,
            grid=(own.shape[1] // step,),
            in_specs=specs,
            out_specs=pl.BlockSpec((PANEL, width), lambda k, place: (0, 0)),
            scratch_shapes=[pltpu.VMEM((2 * step, width), BF16)],
        ),
        compiler_params=pltpu.CompilerParams(vmem_limit_bytes=24 * MIB),
        cost_estimate=pl.CostEstimate(
            flops=PANEL * PANEL * width, bytes_accessed=4 * PANEL * width, transcendentals=0
        ),
    )(*args)


def inverse_kernel(head_ref, out_ref, pair_ref):
    size = PANEL
    rows = lax.broadcasted_iota(jnp.int32, (size, size), 0)
    cols = lax.broadcasted_iota(jnp.int32, (size, size), 1)
    eye = jnp.where(rows == cols, 1.0, 0.0).astype(F32)
    head = head_ref[...]
    damping = 0.01 * (jnp.sum(head * eye) / size)
    block = head + damping * eye
    high = jnp.max(jnp.sum(jnp.abs(block), axis=0))
    start = 2.0 / (high + damping)
    spread = (high - damping) / (high + damping)
    pair_ref[:size] = start * eye
    pair_ref[size:] = start * block

    def more(spread):
        return spread > 1e-3

    def step(spread):
        square = spread * spread
        gain = 2.0 / (2.0 - square)
        turn = gain * (2.0 * eye - pair_ref[size:])
        pair_ref[...] = dot_high(pair_ref[...], turn)
        return square / (2.0 - square)

    lax.while_loop(more, step, spread)
    out = pair_ref[:size]
    for _ in range(2):
        out = out + dot_high(out, eye - dot_high(block, out))
    out_ref[...] = out


def invert(head):
    return pl.pallas_call(
        inverse_kernel,
        out_shape=jax.ShapeDtypeStruct((PANEL, PANEL), F32),
        scratch_shapes=[pltpu.VMEM((2 * PANEL, PANEL), F32)],
        compiler_params=pltpu.CompilerParams(vmem_limit_bytes=8 * MIB),
        cost_estimate=pl.CostEstimate(
            flops=2 * PANEL**3, bytes_accessed=8 * PANEL * PANEL, transcendentals=0
        ),
    )(head)


def gains_kernel(place_ref, inverse_ref, first_ref, second_ref, third_ref, high_ref, pair_ref):
    total = first_ref[...] + second_ref[...] + third_ref[...]
    gains = dot_high(inverse_ref[...], total)
    rows = lax.broadcasted_iota(jnp.int32, gains.shape, 0)
    cols = lax.broadcasted_iota(jnp.int32, gains.shape, 1) + place_ref[0]
    gains = jnp.where(cols < PANEL, jnp.where(rows == cols, -1.0, 0.0), gains)
    high = gains.astype(BF16)
    high_ref[...] = high
    pair_ref[:PANEL] = high
    pair_ref[PANEL:] = (gains - high.astype(F32)).astype(BF16)


def make_gains(inverse, parts, start):
    width = parts[0].shape[1]
    vmem = pl.BlockSpec(memory_space=pltpu.VMEM)
    return pl.pallas_call(
        gains_kernel,
        out_shape=(
            jax.ShapeDtypeStruct((PANEL, width), BF16),
            jax.ShapeDtypeStruct((2 * PANEL, width), BF16),
        ),
        in_specs=[pl.BlockSpec(memory_space=pltpu.SMEM)] + [vmem] * 4,
        compiler_params=pltpu.CompilerParams(vmem_limit_bytes=8 * MIB),
        cost_estimate=pl.CostEstimate(
            flops=12 * PANEL * PANEL * width, bytes_accessed=16 * PANEL * width, transcendentals=0
        ),
    )(start.reshape(1).astype(jnp.int32), inverse, *parts)


def update_kernel(shapes, place_ref, error_ref, weights_ref, *refs):
    count = len(shapes)
    groups, at = [], 0
    for pieces in shapes:
        groups.append(refs[at : at + len(pieces)])
        at += len(pieces)
    out_ref, read_ref, made_ref, read_sems, made_sems = refs[-5:]
    _, parts, step, width = read_ref.shape

    def window(ref, j, i):
        col = pl.multiple_of(place_ref[j] * width, QBLOCK)
        return ref.at[pl.ds(i * step, step), pl.ds(col, width)]

    def read(j, i):
        return pltpu.make_async_copy(window(weights_ref, j, i), read_ref.at[j, i], read_sems.at[j, i])

    def made(j, i):
        return pltpu.make_async_copy(made_ref.at[j, i], window(out_ref, j, i), made_sems.at[j, i])

    spots = [(j, i) for j in range(count) for i in range(parts)]
    for j, i in spots:
        read(j, i).start()
    for j, i in spots:
        read(j, i).wait()
        error = error_ref[i * step : (i + 1) * step, :]
        total = read_ref[j, i].astype(F32)
        row = 0
        for gain in groups[j]:
            for top in range(0, gain.shape[0], PANEL):
                size = min(PANEL, gain.shape[0])
                total += jnp.dot(
                    error[:, row : row + size],
                    gain[top : top + size, :],
                    preferred_element_type=F32,
                )
                row = (row + size) % PANEL
        made_ref[j, i] = total.astype(BF16)
        made(j, i).start()
    for j, i in spots:
        made(j, i).wait()


def update_blocks(out, weights, error, gains, spots):
    rows, cols = weights.shape
    width = gains[0][0].shape[1]
    count = len(gains)
    if width % QBLOCK or width < PANEL:
        out = jnp.zeros_like(weights) if out is None else out
        for pieces, col in zip(gains, spots):
            total = lax.dynamic_slice_in_dim(weights, col * width, width, 1).astype(F32)
            gain = jnp.concatenate(pieces, axis=0)
            for at in range(0, gain.shape[0], PANEL):
                total += jnp.dot(error, gain[at : at + PANEL], preferred_element_type=F32)
            out = lax.dynamic_update_slice_in_dim(out, total.astype(BF16), col * width, 1)
        return out
    parts = 4 if rows % 64 == 0 else 1
    place = jnp.stack(spots).astype(jnp.int32)
    flat = [piece for pieces in gains for piece in pieces]
    vmem, anywhere = pl.BlockSpec(memory_space=pltpu.VMEM), pl.BlockSpec(memory_space=pl.ANY)
    specs = [pl.BlockSpec(memory_space=pltpu.SMEM), vmem, anywhere] + [vmem] * len(flat)
    args = [place, error, weights, *flat]
    aliases = {}
    if out is not None:
        specs.append(anywhere)
        aliases = {len(args): 0}
        args.append(out)
    buffer = pltpu.VMEM((count, parts, rows // parts, width), BF16)
    sems = pltpu.SemaphoreType.DMA((count, parts))
    return pl.pallas_call(
        functools.partial(update_kernel, [[p.shape for p in pieces] for pieces in gains]),
        out_shape=jax.ShapeDtypeStruct((rows, cols), BF16),
        in_specs=specs,
        out_specs=anywhere,
        scratch_shapes=[buffer, buffer, sems, sems],
        input_output_aliases=aliases,
        compiler_params=pltpu.CompilerParams(vmem_limit_bytes=52 * MIB),
        cost_estimate=pl.CostEstimate(
            flops=2 * rows * width * PANEL * count,
            bytes_accessed=4 * rows * width * count,
            transcendentals=0,
        ),
    )(*args)


def swap(x, axis, bit):
    size = lax.axis_size(axis)
    return lax.ppermute(x, axis, [(i, i ^ bit) for i in range(size)])


def hop(x, axis, start):
    return lax.ppermute(x, axis, [(start, start + 1)])


def after(x, *others):
    return lax.optimization_barrier((x, *others))[0]


def dot(left, right):
    return jnp.dot(left, right, preferred_element_type=F32)


def shards(quantized, exponents, weights, keep_mask):
    tokens, cols = quantized.shape
    toks, rows, feats = lax.axis_size("tok"), lax.axis_size("row"), lax.axis_size("feat")
    tok, row, feat = lax.axis_index("tok"), lax.axis_index("row"), lax.axis_index("feat")
    width = cols // (toks * rows)
    root = feat == 0
    hops = feats - 1

    piece = tokens // rows // ROUNDS
    got = [
        [panel_piece(quantized, exponents, row * ROUNDS + c, piece)] for c in range(ROUNDS)
    ]
    for c in range(ROUNDS):
        got[c].append(hop(got[c][0], "feat", 0))

    def settle(parts):
        result = parts[0]
        for h in range(hops):
            result = jnp.where(feat == h + 1, parts[h + 1], result)
        return result

    events = sorted((5 * (c + 1) + 8 * h, c, h) for c in range(ROUNDS) for h in range(hops))
    early = ROUNDS // 2
    full, swapped, token, errors, begun, scale_pad = [], [], got[-1][0], None, {}, None

    def gram(k, first, last, link, extra=None):
        own = jnp.concatenate(full[first:last], axis=1)
        other = jnp.concatenate(swapped[first:last], axis=1)
        col = row * toks + (tok ^ k)
        if link is not None:
            col = after(col, link)
        return gram_block(quantized, scale_pad, own, other, row, col, width, first, extra)

    for _, c, h in events:
        x = got[c][h + 1]
        if token is not None:
            x = after(x, token)
        if h + 1 == hops and c > 1:
            x = after(x, swapped[c - 2])
        got[c][h + 1] = token = x
        if h + 1 < hops:
            got[c].append(hop(x, "feat", h + 1))
        else:
            full.append(settle(got[c]))
            swapped.append(swap(full[-1], "row", 1))
        if (c, h) == (1, 0):
            scale = jnp.exp2(after(exponents, x).astype(F32))
            scale_pad = jnp.pad(scale, ((0, 0), (0, -scale.shape[1] % QBLOCK)))
        elif (c, h) == (0, 1):
            panel_weights, mask = after(weights[:, :PANEL], x), after(keep_mask, x)
            error = jnp.where(mask == 0, panel_weights, jnp.zeros((), BF16))
        elif (c, h) == (ROUNDS - 1, 1):
            errors = [after(error, x)]
            errors.append(hop(errors[0], "feat", 0))
    begun[3] = gram(3, 0, early, full[-1])
    begun[2] = gram(2, 0, early, begun[3])
    swapped[-1] = after(swapped[-1], begun[2], errors[1])
    own, other = jnp.concatenate(full, axis=1), jnp.concatenate(swapped, axis=1)

    head = sum(
        lax.dot_general(x, x, (((1,), (1,)), ((), ())), preferred_element_type=F32)
        for x in (own, other)
    )
    head = head + swap(head, "tok", 1)
    block3 = gram(3, early, ROUNDS, head, begun[3])
    from3 = swap(block3, "tok", 1)
    errors[1] = after(errors[1], block3)
    errors.append(hop(errors[1], "feat", 1))
    head = head + swap(head, "tok", 2)
    block2 = gram(2, early, ROUNDS, from3, begun[2] + from3)
    block2, head = lax.optimization_barrier((block2, head))
    fromx = swap(block2, "tok", 2)
    block1 = gram(1, 0, ROUNDS, block2)
    from1 = swap(block1, "tok", 1)
    errors[2] = after(errors[2], block1)
    for h in range(2, hops):
        errors.append(hop(errors[h], "feat", h))
    block0 = gram(0, 0, ROUNDS, block1)
    inverse = invert(after(head, block0))
    inverse, last = lax.optimization_barrier((inverse, errors[-1]))
    error = settle(errors[:-1] + [last])
    start = jnp.where(root, (row * toks + tok) * width, PANEL)
    high, pair = make_gains(inverse, (block0, from1, fromx), start)

    half = PANEL // 2

    def update(out, group):
        spots = [(row ^ row_bit) * toks + (tok ^ tok_bits) for _, tok_bits, row_bit in group]
        return update_blocks(out, weights, error, [gain for gain, _, _ in group], spots)

    in_x, in_y = swap(high, "tok", 2), swap(high, "row", 1)
    near = swap(pair, "tok", 1)
    out = update(None, [((pair,), 0, 0), ((near,), 1, 0)])
    in_x, in_y, out = lax.optimization_barrier((in_x, in_y, out))
    top, bottom, out = lax.optimization_barrier((in_y[:half], in_x[half:], out))
    far = [swap(top, "tok", 2), swap(bottom, "row", 1)]
    near_x, near_y = swap(in_x, "tok", 1), swap(in_y, "tok", 1)
    out = update(after(out, near_x, near_y), [((in_x,), 2, 0), ((in_y,), 0, 1)])
    far[0], far[1], out = lax.optimization_barrier((far[0], far[1], out))
    near_far = tuple(swap(x, "tok", 1) for x in far)
    last = [((near_x,), 3, 0), ((near_y,), 1, 1), (tuple(far), 2, 1), (near_far, 3, 1)]
    return update(out, last)


def solution(mesh):
    placed = (
        P("tok", "feat"),
        P("tok", "feat"),
        P(("tok", "row"), "feat"),
        P(("tok", "row"), None),
    )
    return jax.shard_map(
        shards, mesh=mesh, in_specs=placed, out_specs=P(("tok", "row"), "feat"), check_vma=False
    )
```

```python
import functools

import jax
import jax.numpy as jnp
from jax import lax
from jax.experimental import pallas as pl
from jax.experimental.pallas import tpu as pltpu
from jax.sharding import PartitionSpec as P

PANEL = 256
QBLOCK = 128
ROUNDS = 4
F32 = jnp.float32
BF16 = jnp.bfloat16
MIB = 1 << 20


def dot_high(left, right):
    return jnp.dot(left, right, precision=lax.Precision.HIGHEST, preferred_element_type=F32)


def panel_kernel(place_ref, quant_ref, exps_ref, out_ref):
    scale = jnp.exp2(exps_ref[:, : PANEL // QBLOCK].astype(F32))
    rows = scale.shape[0]
    wide = [
        jnp.broadcast_to(scale[:, c : c + 1], (rows, QBLOCK)) for c in range(PANEL // QBLOCK)
    ]
    acts = quant_ref[...].astype(F32) * jnp.concatenate(wide, axis=1)
    out_ref[...] = acts.T.astype(BF16)


def panel_piece(quantized, exponents, at, piece):
    blocks = exponents.shape[1]
    return pl.pallas_call(
        panel_kernel,
        out_shape=jax.ShapeDtypeStruct((PANEL, piece), BF16),
        grid_spec=pltpu.PrefetchScalarGridSpec(
            num_scalar_prefetch=1,
            grid=(1,),
            in_specs=[
                pl.BlockSpec((piece, PANEL), lambda i, place: (place[0], 0)),
                pl.BlockSpec((piece, blocks), lambda i, place: (place[0], 0)),
            ],
            out_specs=pl.BlockSpec((PANEL, piece), lambda i, place: (0, 0)),
        ),
        compiler_params=pltpu.CompilerParams(vmem_limit_bytes=8 * MIB),
        cost_estimate=pl.CostEstimate(
            flops=piece * PANEL, bytes_accessed=4 * piece * PANEL, transcendentals=0
        ),
    )(at.reshape(1).astype(jnp.int32), quantized, exponents)


def gram_kernel(blocks, place_ref, *refs):
    acts_ref, out_ref = refs[-1], refs[-2]
    step, width = refs[0].shape
    shift = lax.rem(QBLOCK - lax.rem(place_ref[1] * blocks, QBLOCK), QBLOCK)

    @pl.when(pl.program_id(0) == 0)
    def _():
        out_ref[...] = sum((ref[...] for ref in refs[6:-2]), jnp.zeros_like(out_ref))

    for side in range(2):
        quant_ref, scale_ref, _ = refs[3 * side : 3 * side + 3]
        scale = pltpu.roll(scale_ref[...], shift, 1)
        rows = slice(side * step, (side + 1) * step)
        for c in range(blocks):
            span = slice(c * QBLOCK, (c + 1) * QBLOCK)
            wide = jnp.broadcast_to(scale[:, c : c + 1], (step, QBLOCK)).astype(BF16)
            acts_ref[rows, span] = quant_ref[:, span] * wide
    panel = jnp.concatenate([refs[2][...], refs[5][...]], axis=1)
    out_ref[...] += jnp.dot(panel, acts_ref[...], preferred_element_type=F32)


def gram_block(quantized, scale_pad, own, other, row, col, width, first, *extras):
    tokens, cols = quantized.shape
    if width % QBLOCK or cols // QBLOCK > QBLOCK:
        total = sum(extras)
        for side, panel in enumerate((own, other)):
            at = (row + side) % 2 * (tokens // 2) + first * (tokens // 2 // ROUNDS)
            size = (panel.shape[1], width)
            quant = lax.dynamic_slice(quantized, (at, col * width), size)
            scale = lax.dynamic_slice_in_dim(scale_pad, at, size[0], 0).astype(BF16)
            acts = quant * jnp.take(scale, (col * width + jnp.arange(width)) // QBLOCK, axis=1)
            total = total + jnp.dot(panel, acts, preferred_element_type=F32)
        return total
    step = tokens // 2 // ROUNDS
    place = jnp.stack([row, col]).astype(jnp.int32)
    specs, args = [], [place]
    for side, panel in enumerate((own, other)):

        def at(k, place, side=side):
            return lax.rem(place[0] + side, 2) * ROUNDS + first + k

        specs += [
            pl.BlockSpec((step, width), lambda k, place, at=at: (at(k, place), place[1])),
            pl.BlockSpec((step, QBLOCK), lambda k, place, at=at: (at(k, place), 0)),
            pl.BlockSpec((PANEL, step), lambda k, place: (0, k)),
        ]
        args += [quantized, scale_pad, panel]
    specs += [pl.BlockSpec((PANEL, width), lambda k, place: (0, 0))] * len(extras)
    args += extras
    return pl.pallas_call(
        functools.partial(gram_kernel, width // QBLOCK),
        out_shape=jax.ShapeDtypeStruct((PANEL, width), F32),
        grid_spec=pltpu.PrefetchScalarGridSpec(
            num_scalar_prefetch=1,
            grid=(own.shape[1] // step,),
            in_specs=specs,
            out_specs=pl.BlockSpec((PANEL, width), lambda k, place: (0, 0)),
            scratch_shapes=[pltpu.VMEM((2 * step, width), BF16)],
        ),
        compiler_params=pltpu.CompilerParams(vmem_limit_bytes=24 * MIB),
        cost_estimate=pl.CostEstimate(
            flops=PANEL * PANEL * width, bytes_accessed=4 * PANEL * width, transcendentals=0
        ),
    )(*args)


def inverse_kernel(head_ref, out_ref, pair_ref):
    size = PANEL
    rows = lax.broadcasted_iota(jnp.int32, (size, size), 0)
    cols = lax.broadcasted_iota(jnp.int32, (size, size), 1)
    eye = jnp.where(rows == cols, 1.0, 0.0).astype(F32)
    head = head_ref[...]
    damping = 0.01 * (jnp.sum(head * eye) / size)
    block = head + damping * eye
    high = jnp.max(jnp.sum(jnp.abs(block), axis=0))
    start = 2.0 / (high + damping)
    spread = (high - damping) / (high + damping)
    pair_ref[:size] = start * eye
    pair_ref[size:] = start * block

    def more(spread):
        return spread > 1e-3

    def step(spread):
        square = spread * spread
        gain = 2.0 / (2.0 - square)
        turn = gain * (2.0 * eye - pair_ref[size:])
        pair_ref[...] = dot_high(pair_ref[...], turn)
        return square / (2.0 - square)

    lax.while_loop(more, step, spread)
    out = pair_ref[:size]
    for _ in range(2):
        out = out + dot_high(out, eye - dot_high(block, out))
    out_ref[...] = out


def invert(head):
    return pl.pallas_call(
        inverse_kernel,
        out_shape=jax.ShapeDtypeStruct((PANEL, PANEL), F32),
        scratch_shapes=[pltpu.VMEM((2 * PANEL, PANEL), F32)],
        compiler_params=pltpu.CompilerParams(vmem_limit_bytes=8 * MIB),
        cost_estimate=pl.CostEstimate(
            flops=2 * PANEL**3, bytes_accessed=8 * PANEL * PANEL, transcendentals=0
        ),
    )(head)


def gains_kernel(place_ref, inverse_ref, first_ref, second_ref, third_ref, high_ref, pair_ref):
    total = first_ref[...] + second_ref[...] + third_ref[...]
    gains = dot_high(inverse_ref[...], total)
    rows = lax.broadcasted_iota(jnp.int32, gains.shape, 0)
    cols = lax.broadcasted_iota(jnp.int32, gains.shape, 1) + place_ref[0]
    gains = jnp.where(cols < PANEL, jnp.where(rows == cols, -1.0, 0.0), gains)
    high = gains.astype(BF16)
    high_ref[...] = high
    pair_ref[:PANEL] = high
    pair_ref[PANEL:] = (gains - high.astype(F32)).astype(BF16)


def make_gains(inverse, parts, start):
    width = parts[0].shape[1]
    vmem = pl.BlockSpec(memory_space=pltpu.VMEM)
    return pl.pallas_call(
        gains_kernel,
        out_shape=(
            jax.ShapeDtypeStruct((PANEL, width), BF16),
            jax.ShapeDtypeStruct((2 * PANEL, width), BF16),
        ),
        in_specs=[pl.BlockSpec(memory_space=pltpu.SMEM)] + [vmem] * 4,
        compiler_params=pltpu.CompilerParams(vmem_limit_bytes=8 * MIB),
        cost_estimate=pl.CostEstimate(
            flops=12 * PANEL * PANEL * width, bytes_accessed=16 * PANEL * width, transcendentals=0
        ),
    )(start.reshape(1).astype(jnp.int32), inverse, *parts)


def update_kernel(shapes, place_ref, error_ref, weights_ref, *refs):
    count = len(shapes)
    groups, at = [], 0
    for pieces in shapes:
        groups.append(refs[at : at + len(pieces)])
        at += len(pieces)
    out_ref, read_ref, made_ref, read_sems, made_sems = refs[-5:]
    _, parts, step, width = read_ref.shape

    def window(ref, j, i):
        col = pl.multiple_of(place_ref[j] * width, QBLOCK)
        return ref.at[pl.ds(i * step, step), pl.ds(col, width)]

    def read(j, i):
        return pltpu.make_async_copy(window(weights_ref, j, i), read_ref.at[j, i], read_sems.at[j, i])

    def made(j, i):
        return pltpu.make_async_copy(made_ref.at[j, i], window(out_ref, j, i), made_sems.at[j, i])

    spots = [(j, i) for j in range(count) for i in range(parts)]
    for j, i in spots:
        read(j, i).start()
    for j, i in spots:
        read(j, i).wait()
        error = error_ref[i * step : (i + 1) * step, :]
        total = read_ref[j, i].astype(F32)
        row = 0
        for gain in groups[j]:
            for top in range(0, gain.shape[0], PANEL):
                size = min(PANEL, gain.shape[0])
                total += jnp.dot(
                    error[:, row : row + size],
                    gain[top : top + size, :],
                    preferred_element_type=F32,
                )
                row = (row + size) % PANEL
        made_ref[j, i] = total.astype(BF16)
        made(j, i).start()
    for j, i in spots:
        made(j, i).wait()


def update_blocks(out, weights, error, gains, spots):
    rows, cols = weights.shape
    width = gains[0][0].shape[1]
    count = len(gains)
    if width % QBLOCK or width < PANEL:
        out = jnp.zeros_like(weights) if out is None else out
        for pieces, col in zip(gains, spots):
            total = lax.dynamic_slice_in_dim(weights, col * width, width, 1).astype(F32)
            gain = jnp.concatenate(pieces, axis=0)
            for at in range(0, gain.shape[0], PANEL):
                total += jnp.dot(error, gain[at : at + PANEL], preferred_element_type=F32)
            out = lax.dynamic_update_slice_in_dim(out, total.astype(BF16), col * width, 1)
        return out
    parts = 4 if rows % 64 == 0 else 1
    place = jnp.stack(spots).astype(jnp.int32)
    flat = [piece for pieces in gains for piece in pieces]
    vmem, anywhere = pl.BlockSpec(memory_space=pltpu.VMEM), pl.BlockSpec(memory_space=pl.ANY)
    specs = [pl.BlockSpec(memory_space=pltpu.SMEM), vmem, anywhere] + [vmem] * len(flat)
    args = [place, error, weights, *flat]
    aliases = {}
    if out is not None:
        specs.append(anywhere)
        aliases = {len(args): 0}
        args.append(out)
    buffer = pltpu.VMEM((count, parts, rows // parts, width), BF16)
    sems = pltpu.SemaphoreType.DMA((count, parts))
    return pl.pallas_call(
        functools.partial(update_kernel, [[p.shape for p in pieces] for pieces in gains]),
        out_shape=jax.ShapeDtypeStruct((rows, cols), BF16),
        in_specs=specs,
        out_specs=anywhere,
        scratch_shapes=[buffer, buffer, sems, sems],
        input_output_aliases=aliases,
        compiler_params=pltpu.CompilerParams(vmem_limit_bytes=52 * MIB),
        cost_estimate=pl.CostEstimate(
            flops=2 * rows * width * PANEL * count,
            bytes_accessed=4 * rows * width * count,
            transcendentals=0,
        ),
    )(*args)


def swap(x, axis, bit):
    size = lax.axis_size(axis)
    return lax.ppermute(x, axis, [(i, i ^ bit) for i in range(size)])


def hop(x, axis, start):
    return lax.ppermute(x, axis, [(start, start + 1)])


def after(x, *others):
    return lax.optimization_barrier((x, *others))[0]


def dot(left, right):
    return jnp.dot(left, right, preferred_element_type=F32)


def shards(quantized, exponents, weights, keep_mask):
    tokens, cols = quantized.shape
    toks, rows, feats = lax.axis_size("tok"), lax.axis_size("row"), lax.axis_size("feat")
    tok, row, feat = lax.axis_index("tok"), lax.axis_index("row"), lax.axis_index("feat")
    width = cols // (toks * rows)
    root = feat == 0
    hops = feats - 1

    piece = tokens // rows // ROUNDS
    got = [
        [panel_piece(quantized, exponents, row * ROUNDS + c, piece)] for c in range(ROUNDS)
    ]
    for c in range(ROUNDS):
        got[c].append(hop(got[c][0], "feat", 0))

    def settle(parts):
        result = parts[0]
        for h in range(hops):
            result = jnp.where(feat == h + 1, parts[h + 1], result)
        return result

    events = sorted((5 * (c + 1) + 8 * h, c, h) for c in range(ROUNDS) for h in range(hops))
    early = ROUNDS // 2
    full, swapped, token, errors, begun, scale_pad = [], [], got[-1][0], None, {}, None

    def gram(k, first, last, link, *extras):
        own = jnp.concatenate(full[first:last], axis=1)
        other = jnp.concatenate(swapped[first:last], axis=1)
        col = row * toks + (tok ^ k)
        if link is not None:
            col = after(col, link)
        return gram_block(quantized, scale_pad, own, other, row, col, width, first, *extras)

    for _, c, h in events:
        x = got[c][h + 1]
        if token is not None:
            x = after(x, token)
        if h + 1 == hops and c > 0:
            x = after(x, swapped[max(c - 2, 0)])
        got[c][h + 1] = token = x
        if h + 1 < hops:
            got[c].append(hop(x, "feat", h + 1))
        else:
            full.append(settle(got[c]))
            swapped.append(swap(full[-1], "row", 1))
        if (c, h) == (1, 0):
            scale = jnp.exp2(after(exponents, x).astype(F32))
            scale_pad = jnp.pad(scale, ((0, 0), (0, -scale.shape[1] % QBLOCK)))
        elif (c, h) == (0, 1):
            panel_weights, mask = after(weights[:, :PANEL], x), after(keep_mask, x)
            error = jnp.where(mask == 0, panel_weights, jnp.zeros((), BF16))
        elif (c, h) == (ROUNDS - 1, 1):
            errors = [after(error, x)]
            errors.append(hop(errors[0], "feat", 0))
    begun[3] = gram(3, 0, early, full[-1])
    begun[2] = gram(2, 0, early, begun[3])
    swapped[-1] = after(swapped[-1], begun[2], errors[1])
    own, other = jnp.concatenate(full, axis=1), jnp.concatenate(swapped, axis=1)

    head = sum(
        lax.dot_general(x, x, (((1,), (1,)), ((), ())), preferred_element_type=F32)
        for x in (own, other)
    )
    head = head + swap(head, "tok", 1)
    block3 = gram(3, early, ROUNDS, head, begun[3])
    from3 = swap(block3, "tok", 1)
    errors[1] = after(errors[1], block3)
    errors.append(hop(errors[1], "feat", 1))
    head = head + swap(head, "tok", 2)
    block1 = gram(1, 0, ROUNDS, block3)
    from1 = swap(block1, "tok", 1)
    block2 = gram(2, early, ROUNDS, block1, begun[2], from3)
    block2, head = lax.optimization_barrier((block2, head))
    fromx = swap(block2, "tok", 2)
    errors[2] = after(errors[2], block2)
    for h in range(2, hops):
        errors.append(hop(errors[h], "feat", h))
    block0 = gram(0, 0, ROUNDS, block2)
    inverse = invert(after(head, block0))
    inverse, last = lax.optimization_barrier((inverse, errors[-1]))
    error = settle(errors[:-1] + [last])
    start = jnp.where(root, (row * toks + tok) * width, PANEL)
    high, pair = make_gains(inverse, (block0, from1, fromx), start)

    half = PANEL // 2

    def update(out, group):
        spots = [(row ^ row_bit) * toks + (tok ^ tok_bits) for _, tok_bits, row_bit in group]
        return update_blocks(out, weights, error, [gain for gain, _, _ in group], spots)

    in_x, in_y = swap(high, "tok", 2), swap(high, "row", 1)
    near = swap(pair, "tok", 1)
    out = update(None, [((pair,), 0, 0), ((near,), 1, 0)])
    in_x, in_y, out = lax.optimization_barrier((in_x, in_y, out))
    top, bottom, out = lax.optimization_barrier((in_y[:half], in_x[half:], out))
    far = [swap(top, "tok", 2), swap(bottom, "row", 1)]
    near_x, near_y = swap(in_x, "tok", 1), swap(in_y, "tok", 1)
    middle = [((in_x,), 2, 0), ((in_y,), 0, 1), ((near_x,), 3, 0), ((near_y,), 1, 1)]
    out = update(out, middle)
    far[0], far[1], out = lax.optimization_barrier((far[0], far[1], out))
    near_far = tuple(swap(x, "tok", 1) for x in far)
    return update(out, [(tuple(far), 2, 1), (near_far, 3, 1)])


def solution(mesh):
    placed = (
        P("tok", "feat"),
        P("tok", "feat"),
        P(("tok", "row"), "feat"),
        P(("tok", "row"), None),
    )
    return jax.shard_map(
        shards, mesh=mesh, in_specs=placed, out_specs=P(("tok", "row"), "feat"), check_vma=False
    )
```

```python
import functools

import jax
import jax.numpy as jnp
from jax import lax
from jax.experimental import pallas as pl
from jax.experimental.pallas import tpu as pltpu
from jax.sharding import PartitionSpec as P

PANEL = 256
QBLOCK = 128
ROUNDS = 4
F32 = jnp.float32
BF16 = jnp.bfloat16
MIB = 1 << 20


def dot_high(left, right):
    return jnp.dot(left, right, precision=lax.Precision.HIGHEST, preferred_element_type=F32)


def panel_kernel(place_ref, quant_ref, exps_ref, out_ref):
    scale = jnp.exp2(exps_ref[:, : PANEL // QBLOCK].astype(F32))
    rows = scale.shape[0]
    wide = [
        jnp.broadcast_to(scale[:, c : c + 1], (rows, QBLOCK)) for c in range(PANEL // QBLOCK)
    ]
    acts = quant_ref[...].astype(F32) * jnp.concatenate(wide, axis=1)
    out_ref[...] = acts.T.astype(BF16)


def panel_piece(quantized, exponents, at, piece):
    blocks = exponents.shape[1]
    return pl.pallas_call(
        panel_kernel,
        out_shape=jax.ShapeDtypeStruct((PANEL, piece), BF16),
        grid_spec=pltpu.PrefetchScalarGridSpec(
            num_scalar_prefetch=1,
            grid=(1,),
            in_specs=[
                pl.BlockSpec((piece, PANEL), lambda i, place: (place[0], 0)),
                pl.BlockSpec((piece, blocks), lambda i, place: (place[0], 0)),
            ],
            out_specs=pl.BlockSpec((PANEL, piece), lambda i, place: (0, 0)),
        ),
        compiler_params=pltpu.CompilerParams(vmem_limit_bytes=8 * MIB),
        cost_estimate=pl.CostEstimate(
            flops=piece * PANEL, bytes_accessed=4 * piece * PANEL, transcendentals=0
        ),
    )(at.reshape(1).astype(jnp.int32), quantized, exponents)


def gram_kernel(blocks, place_ref, *refs):
    acts_ref, out_ref = refs[-1], refs[-2]
    step, width = refs[0].shape
    shift = lax.rem(QBLOCK - lax.rem(place_ref[1] * blocks, QBLOCK), QBLOCK)

    @pl.when(pl.program_id(0) == 0)
    def _():
        out_ref[...] = sum((ref[...] for ref in refs[6:-2]), jnp.zeros_like(out_ref))

    for side in range(2):
        quant_ref, scale_ref, _ = refs[3 * side : 3 * side + 3]
        scale = pltpu.roll(scale_ref[...], shift, 1)
        rows = slice(side * step, (side + 1) * step)
        for c in range(blocks):
            span = slice(c * QBLOCK, (c + 1) * QBLOCK)
            wide = jnp.broadcast_to(scale[:, c : c + 1], (step, QBLOCK)).astype(BF16)
            acts_ref[rows, span] = quant_ref[:, span] * wide
    panel = jnp.concatenate([refs[2][...], refs[5][...]], axis=1)
    out_ref[...] += jnp.dot(panel, acts_ref[...], preferred_element_type=F32)


def gram_block(quantized, scale_pad, own, other, row, col, width, first, *extras):
    tokens, cols = quantized.shape
    if width % QBLOCK or cols // QBLOCK > QBLOCK:
        total = sum(extras)
        for side, panel in enumerate((own, other)):
            at = (row + side) % 2 * (tokens // 2) + first * (tokens // 2 // ROUNDS)
            size = (panel.shape[1], width)
            quant = lax.dynamic_slice(quantized, (at, col * width), size)
            scale = lax.dynamic_slice_in_dim(scale_pad, at, size[0], 0).astype(BF16)
            acts = quant * jnp.take(scale, (col * width + jnp.arange(width)) // QBLOCK, axis=1)
            total = total + jnp.dot(panel, acts, preferred_element_type=F32)
        return total
    step = tokens // 2 // ROUNDS
    place = jnp.stack([row, col]).astype(jnp.int32)
    specs, args = [], [place]
    for side, panel in enumerate((own, other)):

        def at(k, place, side=side):
            return lax.rem(place[0] + side, 2) * ROUNDS + first + k

        specs += [
            pl.BlockSpec((step, width), lambda k, place, at=at: (at(k, place), place[1])),
            pl.BlockSpec((step, QBLOCK), lambda k, place, at=at: (at(k, place), 0)),
            pl.BlockSpec((PANEL, step), lambda k, place: (0, k)),
        ]
        args += [quantized, scale_pad, panel]
    specs += [pl.BlockSpec((PANEL, width), lambda k, place: (0, 0))] * len(extras)
    args += extras
    return pl.pallas_call(
        functools.partial(gram_kernel, width // QBLOCK),
        out_shape=jax.ShapeDtypeStruct((PANEL, width), F32),
        grid_spec=pltpu.PrefetchScalarGridSpec(
            num_scalar_prefetch=1,
            grid=(own.shape[1] // step,),
            in_specs=specs,
            out_specs=pl.BlockSpec((PANEL, width), lambda k, place: (0, 0)),
            scratch_shapes=[pltpu.VMEM((2 * step, width), BF16)],
        ),
        compiler_params=pltpu.CompilerParams(vmem_limit_bytes=24 * MIB),
        cost_estimate=pl.CostEstimate(
            flops=PANEL * PANEL * width, bytes_accessed=4 * PANEL * width, transcendentals=0
        ),
    )(*args)


def inverse_kernel(head_ref, out_ref, pair_ref):
    size = PANEL
    rows = lax.broadcasted_iota(jnp.int32, (size, size), 0)
    cols = lax.broadcasted_iota(jnp.int32, (size, size), 1)
    eye = jnp.where(rows == cols, 1.0, 0.0).astype(F32)
    head = head_ref[...]
    damping = 0.01 * (jnp.sum(head * eye) / size)
    block = head + damping * eye
    high = jnp.max(jnp.sum(jnp.abs(block), axis=0))
    start = 2.0 / (high + damping)
    spread = (high - damping) / (high + damping)
    pair_ref[:size] = start * eye
    pair_ref[size:] = start * block

    def more(spread):
        return spread > 1e-3

    def step(spread):
        square = spread * spread
        gain = 2.0 / (2.0 - square)
        turn = gain * (2.0 * eye - pair_ref[size:])
        pair_ref[...] = dot_high(pair_ref[...], turn)
        return square / (2.0 - square)

    lax.while_loop(more, step, spread)
    out = pair_ref[:size]
    for _ in range(2):
        out = out + dot_high(out, eye - dot_high(block, out))
    out_ref[...] = out


def invert(head):
    return pl.pallas_call(
        inverse_kernel,
        out_shape=jax.ShapeDtypeStruct((PANEL, PANEL), F32),
        scratch_shapes=[pltpu.VMEM((2 * PANEL, PANEL), F32)],
        compiler_params=pltpu.CompilerParams(vmem_limit_bytes=8 * MIB),
        cost_estimate=pl.CostEstimate(
            flops=2 * PANEL**3, bytes_accessed=8 * PANEL * PANEL, transcendentals=0
        ),
    )(head)


def gains_kernel(place_ref, inverse_ref, first_ref, second_ref, third_ref, high_ref, pair_ref):
    total = first_ref[...] + second_ref[...] + third_ref[...]
    gains = dot_high(inverse_ref[...], total)
    rows = lax.broadcasted_iota(jnp.int32, gains.shape, 0)
    cols = lax.broadcasted_iota(jnp.int32, gains.shape, 1) + place_ref[0]
    gains = jnp.where(cols < PANEL, jnp.where(rows == cols, -1.0, 0.0), gains)
    high = gains.astype(BF16)
    high_ref[...] = high
    pair_ref[:PANEL] = high
    pair_ref[PANEL:] = (gains - high.astype(F32)).astype(BF16)


def make_gains(inverse, parts, start):
    width = parts[0].shape[1]
    vmem = pl.BlockSpec(memory_space=pltpu.VMEM)
    return pl.pallas_call(
        gains_kernel,
        out_shape=(
            jax.ShapeDtypeStruct((PANEL, width), BF16),
            jax.ShapeDtypeStruct((2 * PANEL, width), BF16),
        ),
        in_specs=[pl.BlockSpec(memory_space=pltpu.SMEM)] + [vmem] * 4,
        compiler_params=pltpu.CompilerParams(vmem_limit_bytes=8 * MIB),
        cost_estimate=pl.CostEstimate(
            flops=12 * PANEL * PANEL * width, bytes_accessed=16 * PANEL * width, transcendentals=0
        ),
    )(start.reshape(1).astype(jnp.int32), inverse, *parts)


def update_kernel(shapes, place_ref, error_ref, weights_ref, *refs):
    count = len(shapes)
    groups, at = [], 0
    for pieces in shapes:
        groups.append(refs[at : at + len(pieces)])
        at += len(pieces)
    out_ref, read_ref, made_ref, read_sems, made_sems = refs[-5:]
    _, parts, step, width = read_ref.shape

    def window(ref, j, i):
        col = pl.multiple_of(place_ref[j] * width, QBLOCK)
        return ref.at[pl.ds(i * step, step), pl.ds(col, width)]

    def read(j, i):
        return pltpu.make_async_copy(window(weights_ref, j, i), read_ref.at[j, i], read_sems.at[j, i])

    def made(j, i):
        return pltpu.make_async_copy(made_ref.at[j, i], window(out_ref, j, i), made_sems.at[j, i])

    spots = [(j, i) for j in range(count) for i in range(parts)]
    for j, i in spots:
        read(j, i).start()
    for j, i in spots:
        read(j, i).wait()
        error = error_ref[i * step : (i + 1) * step, :]
        total = read_ref[j, i].astype(F32)
        row = 0
        for gain in groups[j]:
            for top in range(0, gain.shape[0], PANEL):
                size = min(PANEL, gain.shape[0])
                total += jnp.dot(
                    error[:, row : row + size],
                    gain[top : top + size, :],
                    preferred_element_type=F32,
                )
                row = (row + size) % PANEL
        made_ref[j, i] = total.astype(BF16)
        made(j, i).start()
    for j, i in spots:
        made(j, i).wait()


def update_blocks(out, weights, error, gains, spots):
    rows, cols = weights.shape
    width = gains[0][0].shape[1]
    count = len(gains)
    if width % QBLOCK or width < PANEL:
        out = jnp.zeros_like(weights) if out is None else out
        for pieces, col in zip(gains, spots):
            total = lax.dynamic_slice_in_dim(weights, col * width, width, 1).astype(F32)
            gain = jnp.concatenate(pieces, axis=0)
            for at in range(0, gain.shape[0], PANEL):
                total += jnp.dot(error, gain[at : at + PANEL], preferred_element_type=F32)
            out = lax.dynamic_update_slice_in_dim(out, total.astype(BF16), col * width, 1)
        return out
    parts = 4 if rows % 64 == 0 else 1
    place = jnp.stack(spots).astype(jnp.int32)
    flat = [piece for pieces in gains for piece in pieces]
    vmem, anywhere = pl.BlockSpec(memory_space=pltpu.VMEM), pl.BlockSpec(memory_space=pl.ANY)
    specs = [pl.BlockSpec(memory_space=pltpu.SMEM), vmem, anywhere] + [vmem] * len(flat)
    args = [place, error, weights, *flat]
    aliases = {}
    if out is not None:
        specs.append(anywhere)
        aliases = {len(args): 0}
        args.append(out)
    buffer = pltpu.VMEM((count, parts, rows // parts, width), BF16)
    sems = pltpu.SemaphoreType.DMA((count, parts))
    return pl.pallas_call(
        functools.partial(update_kernel, [[p.shape for p in pieces] for pieces in gains]),
        out_shape=jax.ShapeDtypeStruct((rows, cols), BF16),
        in_specs=specs,
        out_specs=anywhere,
        scratch_shapes=[buffer, buffer, sems, sems],
        input_output_aliases=aliases,
        compiler_params=pltpu.CompilerParams(vmem_limit_bytes=52 * MIB),
        cost_estimate=pl.CostEstimate(
            flops=2 * rows * width * PANEL * count,
            bytes_accessed=4 * rows * width * count,
            transcendentals=0,
        ),
    )(*args)


def swap(x, axis, bit):
    size = lax.axis_size(axis)
    return lax.ppermute(x, axis, [(i, i ^ bit) for i in range(size)])


def hop(x, axis, start):
    return lax.ppermute(x, axis, [(start, start + 1)])


def after(x, *others):
    return lax.optimization_barrier((x, *others))[0]


def dot(left, right):
    return jnp.dot(left, right, preferred_element_type=F32)


def shards(quantized, exponents, weights, keep_mask):
    tokens, cols = quantized.shape
    toks, rows, feats = lax.axis_size("tok"), lax.axis_size("row"), lax.axis_size("feat")
    tok, row, feat = lax.axis_index("tok"), lax.axis_index("row"), lax.axis_index("feat")
    width = cols // (toks * rows)
    root = feat == 0
    hops = feats - 1

    piece = tokens // rows // ROUNDS
    got = [
        [panel_piece(quantized, exponents, row * ROUNDS + c, piece)] for c in range(ROUNDS)
    ]
    for c in range(ROUNDS):
        got[c].append(hop(got[c][0], "feat", 0))

    def settle(parts):
        result = parts[0]
        for h in range(hops):
            result = jnp.where(feat == h + 1, parts[h + 1], result)
        return result

    events = sorted((5 * (c + 1) + 8 * h, c, h) for c in range(ROUNDS) for h in range(hops))
    early = ROUNDS // 2
    full, swapped, token, errors, begun, scale_pad = [], [], got[-1][0], None, {}, None

    def gram(k, first, last, link, *extras):
        own = jnp.concatenate(full[first:last], axis=1)
        other = jnp.concatenate(swapped[first:last], axis=1)
        col = row * toks + (tok ^ k)
        if link is not None:
            col = after(col, link)
        return gram_block(quantized, scale_pad, own, other, row, col, width, first, *extras)

    for _, c, h in events:
        x = got[c][h + 1]
        if token is not None:
            x = after(x, token)
        if h + 1 == hops and c > 1:
            x = after(x, swapped[c - 2])
        got[c][h + 1] = token = x
        if h + 1 < hops:
            got[c].append(hop(x, "feat", h + 1))
        else:
            full.append(settle(got[c]))
            swapped.append(swap(full[-1], "row", 1))
        if (c, h) == (1, 0):
            scale = jnp.exp2(after(exponents, x).astype(F32))
            scale_pad = jnp.pad(scale, ((0, 0), (0, -scale.shape[1] % QBLOCK)))
        elif (c, h) == (0, 1):
            panel_weights, mask = after(weights[:, :PANEL], x), after(keep_mask, x)
            error = jnp.where(mask == 0, panel_weights, jnp.zeros((), BF16))
        elif (c, h) == (ROUNDS - 1, 1):
            errors = [after(error, x)]
            errors.append(hop(errors[0], "feat", 0))
    begun[3] = gram(3, 0, early, full[-1])
    begun[2] = gram(2, 0, early, begun[3])
    swapped[-1] = after(swapped[-1], begun[2], errors[1])
    own, other = jnp.concatenate(full, axis=1), jnp.concatenate(swapped, axis=1)

    head = sum(
        lax.dot_general(x, x, (((1,), (1,)), ((), ())), preferred_element_type=F32)
        for x in (own, other)
    )
    head = head + swap(head, "tok", 1)
    block3 = gram(3, early, ROUNDS, head, begun[3])
    from3 = swap(block3, "tok", 1)
    errors[1] = after(errors[1], block3)
    errors.append(hop(errors[1], "feat", 1))
    head = head + swap(head, "tok", 2)
    block1 = gram(1, 0, ROUNDS, block3)
    from1 = swap(block1, "tok", 1)
    block2 = gram(2, early, ROUNDS, block1, begun[2], from3)
    block2, head = lax.optimization_barrier((block2, head))
    fromx = swap(block2, "tok", 2)
    errors[2] = after(errors[2], block2)
    for h in range(2, hops):
        errors.append(hop(errors[h], "feat", h))
    block0 = gram(0, 0, ROUNDS, block2)
    inverse = invert(after(head, block0))
    inverse, last = lax.optimization_barrier((inverse, errors[-1]))
    error = settle(errors[:-1] + [last])
    start = jnp.where(root, (row * toks + tok) * width, PANEL)
    high, pair = make_gains(inverse, (block0, from1, fromx), start)

    half = PANEL // 2

    def update(out, group):
        spots = [(row ^ row_bit) * toks + (tok ^ tok_bits) for _, tok_bits, row_bit in group]
        return update_blocks(out, weights, error, [gain for gain, _, _ in group], spots)

    in_x, in_y = swap(high, "tok", 2), swap(high, "row", 1)
    near = swap(pair, "tok", 1)
    out = update(None, [((pair,), 0, 0), ((near,), 1, 0)])
    in_x, in_y, out = lax.optimization_barrier((in_x, in_y, out))
    top, bottom, out = lax.optimization_barrier((in_y[:half], in_x[half:], out))
    far = [swap(top, "tok", 2), swap(bottom, "row", 1)]
    near_x, near_y = swap(in_x, "tok", 1), swap(in_y, "tok", 1)
    middle = [((in_x,), 2, 0), ((in_y,), 0, 1), ((near_x,), 3, 0), ((near_y,), 1, 1)]
    out = update(out, middle)
    far[0], far[1], out = lax.optimization_barrier((far[0], far[1], out))
    near_far = tuple(swap(x, "tok", 1) for x in far)
    return update(out, [(tuple(far), 2, 1), (near_far, 3, 1)])


def solution(mesh):
    placed = (
        P("tok", "feat"),
        P("tok", "feat"),
        P(("tok", "row"), "feat"),
        P(("tok", "row"), None),
    )
    return jax.shard_map(
        shards, mesh=mesh, in_specs=placed, out_specs=P(("tok", "row"), "feat"), check_vma=False
    )
```

```python
import functools

import jax
import jax.numpy as jnp
from jax import lax
from jax.experimental import pallas as pl
from jax.experimental.pallas import tpu as pltpu
from jax.sharding import PartitionSpec as P

PANEL = 256
QBLOCK = 128
ROUNDS = 4
F32 = jnp.float32
BF16 = jnp.bfloat16
MIB = 1 << 20


def dot_high(left, right):
    return jnp.dot(left, right, precision=lax.Precision.HIGHEST, preferred_element_type=F32)


def panel_kernel(place_ref, quant_ref, exps_ref, out_ref):
    scale = jnp.exp2(exps_ref[:, : PANEL // QBLOCK].astype(F32))
    rows = scale.shape[0]
    wide = [
        jnp.broadcast_to(scale[:, c : c + 1], (rows, QBLOCK)) for c in range(PANEL // QBLOCK)
    ]
    acts = quant_ref[...].astype(F32) * jnp.concatenate(wide, axis=1)
    out_ref[...] = acts.T.astype(BF16)


def panel_piece(quantized, exponents, at, piece):
    blocks = exponents.shape[1]
    return pl.pallas_call(
        panel_kernel,
        out_shape=jax.ShapeDtypeStruct((PANEL, piece), BF16),
        grid_spec=pltpu.PrefetchScalarGridSpec(
            num_scalar_prefetch=1,
            grid=(1,),
            in_specs=[
                pl.BlockSpec((piece, PANEL), lambda i, place: (place[0], 0)),
                pl.BlockSpec((piece, blocks), lambda i, place: (place[0], 0)),
            ],
            out_specs=pl.BlockSpec((PANEL, piece), lambda i, place: (0, 0)),
        ),
        compiler_params=pltpu.CompilerParams(vmem_limit_bytes=8 * MIB),
        cost_estimate=pl.CostEstimate(
            flops=piece * PANEL, bytes_accessed=4 * piece * PANEL, transcendentals=0
        ),
    )(at.reshape(1).astype(jnp.int32), quantized, exponents)


def gram_kernel(blocks, place_ref, *refs):
    acts_ref, out_ref = refs[-1], refs[-2]
    step, width = refs[0].shape
    shift = lax.rem(QBLOCK - lax.rem(place_ref[1] * blocks, QBLOCK), QBLOCK)

    @pl.when(pl.program_id(0) == 0)
    def _():
        out_ref[...] = sum((ref[...] for ref in refs[6:-2]), jnp.zeros_like(out_ref))

    for side in range(2):
        quant_ref, scale_ref, _ = refs[3 * side : 3 * side + 3]
        scale = pltpu.roll(scale_ref[...], shift, 1)
        rows = slice(side * step, (side + 1) * step)
        for c in range(blocks):
            span = slice(c * QBLOCK, (c + 1) * QBLOCK)
            wide = jnp.broadcast_to(scale[:, c : c + 1], (step, QBLOCK)).astype(BF16)
            acts_ref[rows, span] = quant_ref[:, span] * wide
    panel = jnp.concatenate([refs[2][...], refs[5][...]], axis=1)
    out_ref[...] += jnp.dot(panel, acts_ref[...], preferred_element_type=F32)


def gram_block(quantized, scale_pad, own, other, row, col, width, first, *extras):
    tokens, cols = quantized.shape
    if width % QBLOCK or cols // QBLOCK > QBLOCK:
        total = sum(extras)
        for side, panel in enumerate((own, other)):
            at = (row + side) % 2 * (tokens // 2) + first * (tokens // 2 // ROUNDS)
            size = (panel.shape[1], width)
            quant = lax.dynamic_slice(quantized, (at, col * width), size)
            scale = lax.dynamic_slice_in_dim(scale_pad, at, size[0], 0).astype(BF16)
            acts = quant * jnp.take(scale, (col * width + jnp.arange(width)) // QBLOCK, axis=1)
            total = total + jnp.dot(panel, acts, preferred_element_type=F32)
        return total
    step = tokens // 2 // ROUNDS
    place = jnp.stack([row, col]).astype(jnp.int32)
    specs, args = [], [place]
    for side, panel in enumerate((own, other)):

        def at(k, place, side=side):
            return lax.rem(place[0] + side, 2) * ROUNDS + first + k

        specs += [
            pl.BlockSpec((step, width), lambda k, place, at=at: (at(k, place), place[1])),
            pl.BlockSpec((step, QBLOCK), lambda k, place, at=at: (at(k, place), 0)),
            pl.BlockSpec((PANEL, step), lambda k, place: (0, k)),
        ]
        args += [quantized, scale_pad, panel]
    specs += [pl.BlockSpec((PANEL, width), lambda k, place: (0, 0))] * len(extras)
    args += extras
    return pl.pallas_call(
        functools.partial(gram_kernel, width // QBLOCK),
        out_shape=jax.ShapeDtypeStruct((PANEL, width), F32),
        grid_spec=pltpu.PrefetchScalarGridSpec(
            num_scalar_prefetch=1,
            grid=(own.shape[1] // step,),
            in_specs=specs,
            out_specs=pl.BlockSpec((PANEL, width), lambda k, place: (0, 0)),
            scratch_shapes=[pltpu.VMEM((2 * step, width), BF16)],
        ),
        compiler_params=pltpu.CompilerParams(vmem_limit_bytes=24 * MIB),
        cost_estimate=pl.CostEstimate(
            flops=PANEL * PANEL * width, bytes_accessed=4 * PANEL * width, transcendentals=0
        ),
    )(*args)


def inverse_kernel(head_ref, out_ref, pair_ref):
    size = PANEL
    rows = lax.broadcasted_iota(jnp.int32, (size, size), 0)
    cols = lax.broadcasted_iota(jnp.int32, (size, size), 1)
    eye = jnp.where(rows == cols, 1.0, 0.0).astype(F32)
    head = head_ref[...]
    damping = 0.01 * (jnp.sum(head * eye) / size)
    block = head + damping * eye
    high = jnp.max(jnp.sum(jnp.abs(block), axis=0))
    start = 2.0 / (high + damping)
    spread = (high - damping) / (high + damping)
    pair_ref[:size] = start * eye
    pair_ref[size:] = start * block

    def more(spread):
        return spread > 1e-3

    def step(spread):
        square = spread * spread
        gain = 2.0 / (2.0 - square)
        turn = gain * (2.0 * eye - pair_ref[size:])
        pair_ref[...] = dot_high(pair_ref[...], turn)
        return square / (2.0 - square)

    lax.while_loop(more, step, spread)
    out = pair_ref[:size]
    for _ in range(2):
        out = out + dot_high(out, eye - dot_high(block, out))
    out_ref[...] = out


def invert(head):
    return pl.pallas_call(
        inverse_kernel,
        out_shape=jax.ShapeDtypeStruct((PANEL, PANEL), F32),
        scratch_shapes=[pltpu.VMEM((2 * PANEL, PANEL), F32)],
        compiler_params=pltpu.CompilerParams(vmem_limit_bytes=8 * MIB),
        cost_estimate=pl.CostEstimate(
            flops=2 * PANEL**3, bytes_accessed=8 * PANEL * PANEL, transcendentals=0
        ),
    )(head)


def gains_kernel(place_ref, inverse_ref, first_ref, second_ref, third_ref, high_ref, pair_ref):
    total = first_ref[...] + second_ref[...] + third_ref[...]
    gains = dot_high(inverse_ref[...], total)
    rows = lax.broadcasted_iota(jnp.int32, gains.shape, 0)
    cols = lax.broadcasted_iota(jnp.int32, gains.shape, 1) + place_ref[0]
    gains = jnp.where(cols < PANEL, jnp.where(rows == cols, -1.0, 0.0), gains)
    high = gains.astype(BF16)
    high_ref[...] = high
    pair_ref[:PANEL] = high
    pair_ref[PANEL:] = (gains - high.astype(F32)).astype(BF16)


def make_gains(inverse, parts, start):
    width = parts[0].shape[1]
    vmem = pl.BlockSpec(memory_space=pltpu.VMEM)
    return pl.pallas_call(
        gains_kernel,
        out_shape=(
            jax.ShapeDtypeStruct((PANEL, width), BF16),
            jax.ShapeDtypeStruct((2 * PANEL, width), BF16),
        ),
        in_specs=[pl.BlockSpec(memory_space=pltpu.SMEM)] + [vmem] * 4,
        compiler_params=pltpu.CompilerParams(vmem_limit_bytes=8 * MIB),
        cost_estimate=pl.CostEstimate(
            flops=12 * PANEL * PANEL * width, bytes_accessed=16 * PANEL * width, transcendentals=0
        ),
    )(start.reshape(1).astype(jnp.int32), inverse, *parts)


def update_kernel(shapes, place_ref, error_ref, weights_ref, *refs):
    count = len(shapes)
    groups, at = [], 0
    for pieces in shapes:
        groups.append(refs[at : at + len(pieces)])
        at += len(pieces)
    out_ref, read_ref, made_ref, read_sems, made_sems = refs[-5:]
    _, parts, step, width = read_ref.shape

    def window(ref, j, i):
        col = pl.multiple_of(place_ref[j] * width, QBLOCK)
        return ref.at[pl.ds(i * step, step), pl.ds(col, width)]

    def read(j, i):
        return pltpu.make_async_copy(window(weights_ref, j, i), read_ref.at[j, i], read_sems.at[j, i])

    def made(j, i):
        return pltpu.make_async_copy(made_ref.at[j, i], window(out_ref, j, i), made_sems.at[j, i])

    spots = [(j, i) for j in range(count) for i in range(parts)]
    for j, i in spots:
        read(j, i).start()
    for j, i in spots:
        read(j, i).wait()
        error = error_ref[i * step : (i + 1) * step, :]
        total = read_ref[j, i].astype(F32)
        row = 0
        for gain in groups[j]:
            for top in range(0, gain.shape[0], PANEL):
                size = min(PANEL, gain.shape[0])
                total += jnp.dot(
                    error[:, row : row + size],
                    gain[top : top + size, :],
                    preferred_element_type=F32,
                )
                row = (row + size) % PANEL
        made_ref[j, i] = total.astype(BF16)
        made(j, i).start()
    for j, i in spots:
        made(j, i).wait()


def update_blocks(out, weights, error, gains, spots):
    rows, cols = weights.shape
    width = gains[0][0].shape[1]
    count = len(gains)
    if width % QBLOCK or width < PANEL:
        out = jnp.zeros_like(weights) if out is None else out
        for pieces, col in zip(gains, spots):
            total = lax.dynamic_slice_in_dim(weights, col * width, width, 1).astype(F32)
            gain = jnp.concatenate(pieces, axis=0)
            for at in range(0, gain.shape[0], PANEL):
                total += jnp.dot(error, gain[at : at + PANEL], preferred_element_type=F32)
            out = lax.dynamic_update_slice_in_dim(out, total.astype(BF16), col * width, 1)
        return out
    parts = 4 if rows % 64 == 0 else 1
    place = jnp.stack(spots).astype(jnp.int32)
    flat = [piece for pieces in gains for piece in pieces]
    vmem, anywhere = pl.BlockSpec(memory_space=pltpu.VMEM), pl.BlockSpec(memory_space=pl.ANY)
    specs = [pl.BlockSpec(memory_space=pltpu.SMEM), vmem, anywhere] + [vmem] * len(flat)
    args = [place, error, weights, *flat]
    aliases = {}
    if out is not None:
        specs.append(anywhere)
        aliases = {len(args): 0}
        args.append(out)
    buffer = pltpu.VMEM((count, parts, rows // parts, width), BF16)
    sems = pltpu.SemaphoreType.DMA((count, parts))
    return pl.pallas_call(
        functools.partial(update_kernel, [[p.shape for p in pieces] for pieces in gains]),
        out_shape=jax.ShapeDtypeStruct((rows, cols), BF16),
        in_specs=specs,
        out_specs=anywhere,
        scratch_shapes=[buffer, buffer, sems, sems],
        input_output_aliases=aliases,
        compiler_params=pltpu.CompilerParams(vmem_limit_bytes=52 * MIB),
        cost_estimate=pl.CostEstimate(
            flops=2 * rows * width * PANEL * count,
            bytes_accessed=4 * rows * width * count,
            transcendentals=0,
        ),
    )(*args)


def swap(x, axis, bit):
    size = lax.axis_size(axis)
    return lax.ppermute(x, axis, [(i, i ^ bit) for i in range(size)])


def hop(x, axis, start):
    return lax.ppermute(x, axis, [(start, start + 1)])


def after(x, *others):
    return lax.optimization_barrier((x, *others))[0]


def dot(left, right):
    return jnp.dot(left, right, preferred_element_type=F32)


def shards(quantized, exponents, weights, keep_mask):
    tokens, cols = quantized.shape
    toks, rows, feats = lax.axis_size("tok"), lax.axis_size("row"), lax.axis_size("feat")
    tok, row, feat = lax.axis_index("tok"), lax.axis_index("row"), lax.axis_index("feat")
    width = cols // (toks * rows)
    root = feat == 0
    hops = feats - 1

    piece = tokens // rows // ROUNDS
    got = [
        [panel_piece(quantized, exponents, row * ROUNDS + c, piece)] for c in range(ROUNDS)
    ]
    for c in range(ROUNDS):
        got[c].append(hop(got[c][0], "feat", 0))

    def settle(parts):
        result = parts[0]
        for h in range(hops):
            result = jnp.where(feat == h + 1, parts[h + 1], result)
        return result

    events = sorted((5 * (c + 1) + 8 * h, c, h) for c in range(ROUNDS) for h in range(hops))
    early = ROUNDS // 2
    full, swapped, token, errors, begun, scale_pad = [], [], got[-1][0], None, {}, None

    def gram(k, first, last, link, *extras):
        own = jnp.concatenate(full[first:last], axis=1)
        other = jnp.concatenate(swapped[first:last], axis=1)
        col = row * toks + (tok ^ k)
        if link is not None:
            col = after(col, link)
        return gram_block(quantized, scale_pad, own, other, row, col, width, first, *extras)

    for _, c, h in events:
        x = got[c][h + 1]
        if token is not None:
            x = after(x, token)
        if h + 1 == hops and c > 1:
            x = after(x, swapped[0])
        got[c][h + 1] = token = x
        if h + 1 < hops:
            got[c].append(hop(x, "feat", h + 1))
        else:
            full.append(settle(got[c]))
            swapped.append(swap(full[-1], "row", 1))
        if (c, h) == (1, 0):
            scale = jnp.exp2(after(exponents, x).astype(F32))
            scale_pad = jnp.pad(scale, ((0, 0), (0, -scale.shape[1] % QBLOCK)))
        elif (c, h) == (0, 1):
            panel_weights, mask = after(weights[:, :PANEL], x), after(keep_mask, x)
            error = jnp.where(mask == 0, panel_weights, jnp.zeros((), BF16))
        elif (c, h) == (ROUNDS - 1, 1):
            errors = [after(error, x)]
            errors.append(hop(errors[0], "feat", 0))
    begun[3] = gram(3, 0, early, full[-1])
    begun[2] = gram(2, 0, early, begun[3])
    swapped[-1] = after(swapped[-1], begun[2], errors[1])
    own, other = jnp.concatenate(full, axis=1), jnp.concatenate(swapped, axis=1)

    head = sum(
        lax.dot_general(x, x, (((1,), (1,)), ((), ())), preferred_element_type=F32)
        for x in (own, other)
    )
    head = head + swap(head, "tok", 1)
    block3 = gram(3, early, ROUNDS, head, begun[3])
    from3 = swap(block3, "tok", 1)
    errors[1] = after(errors[1], block3)
    errors.append(hop(errors[1], "feat", 1))
    head = head + swap(head, "tok", 2)
    block1 = gram(1, 0, ROUNDS, block3)
    from1 = swap(block1, "tok", 1)
    block2 = gram(2, early, ROUNDS, block1, begun[2], from3)
    block2, head = lax.optimization_barrier((block2, head))
    fromx = swap(block2, "tok", 2)
    errors[2] = after(errors[2], block2)
    for h in range(2, hops):
        errors.append(hop(errors[h], "feat", h))
    block0 = gram(0, 0, ROUNDS, block2)
    inverse = invert(after(head, block0))
    inverse, last = lax.optimization_barrier((inverse, errors[-1]))
    error = settle(errors[:-1] + [last])
    start = jnp.where(root, (row * toks + tok) * width, PANEL)
    high, pair = make_gains(inverse, (block0, from1, fromx), start)

    half = PANEL // 2

    def update(out, group):
        spots = [(row ^ row_bit) * toks + (tok ^ tok_bits) for _, tok_bits, row_bit in group]
        return update_blocks(out, weights, error, [gain for gain, _, _ in group], spots)

    in_x, in_y = swap(high, "tok", 2), swap(high, "row", 1)
    near = swap(pair, "tok", 1)
    out = update(None, [((pair,), 0, 0), ((near,), 1, 0)])
    in_x, in_y, out = lax.optimization_barrier((in_x, in_y, out))
    top, bottom, out = lax.optimization_barrier((in_y[:half], in_x[half:], out))
    far = [swap(top, "tok", 2), swap(bottom, "row", 1)]
    near_x, near_y = swap(in_x, "tok", 1), swap(in_y, "tok", 1)
    middle = [((in_x,), 2, 0), ((in_y,), 0, 1), ((near_x,), 3, 0), ((near_y,), 1, 1)]
    out = update(out, middle)
    far[0], far[1], out = lax.optimization_barrier((far[0], far[1], out))
    near_far = tuple(swap(x, "tok", 1) for x in far)
    return update(out, [(tuple(far), 2, 1), (near_far, 3, 1)])


def solution(mesh):
    placed = (
        P("tok", "feat"),
        P("tok", "feat"),
        P(("tok", "row"), "feat"),
        P(("tok", "row"), None),
    )
    return jax.shard_map(
        shards, mesh=mesh, in_specs=placed, out_specs=P(("tok", "row"), "feat"), check_vma=False
    )
```
